512 devices in a mesh: ka: 64 (over z, y_lo, core), ga: 8 (over x, y_hi).
Axes of the slice: x: 4, y: 8 (y_hi: 2, y_lo: 4; y = y_hi * 4 + y_lo), z: 8, core: 2. Of those that a mesh axis runs over, the one named last changes fastest.
Arguments:
- wave_fields: bfloat16 [64, 16384, 2, 256], P('ka', 'ga'), may hold values from -6 to 6
- potential_change: bfloat16 [4, 2, 16384], P(None, None, 'ga'), may hold values from -0.046875 to 0.046875
- projectors: bfloat16 [4, 64, 16384], P(None, None, 'ga'), may hold values from -0.046875 to 0.046875
- mode_vectors: float32 [4, 3, 2, 8], replicated, may hold values from -6 to 6
- coupling_base: float32 [64, 64], replicated, may hold values from -4 to 4
- coupling_change: float32 [4, 2, 64, 64], replicated, may hold values from -4 to 4
- projector_atom: int32 [64], replicated, may hold values from 0 to 7, never falling along the last dimension, each value on 1 to 16 neighbouring positions
Outputs:
- matrix_elements: float32 [64, 256, 4, 2, 256], P('ka', 'ga')
The draws below stay inside these ranges and needn't reach their ends.
Inputs may be any that keep to these rules, and one draw needn't show every extreme that they name: `projector_atom`: projectors of one atom stand together and atoms come in ascending order; every atom has 1 to 16 projectors, and some atom has exactly 16.
All inputs are finite; a program needn't handle non-finite values.
Results may differ from the reference program's by a relative error of at most 0.001.
Values may be sent and summed in bfloat16 or wider, within the bound.
A program may use at most 64 MiB of HBM per device.

```python
import math
import jax
import jax.numpy as jnp
import numpy as np
from jax import lax

NB = 256
MODES = 4
ATOMS = 8
P_SIZE = 64
NK = 64
QSTEP = 16
R_TOTAL = 16384


def shard_levels(own_key, extent, pieces, low, high):
    def one(position, parts):
        steps = jax.random.uniform(jax.random.fold_in(jax.random.fold_in(own_key, 6), position), (parts,), jnp.float32, low / len(pieces), high / len(pieces))
        return jnp.repeat(jnp.exp(steps), extent[position] // parts).reshape((-1,) + (1,) * (len(extent) - position - 1))

    gain = one(*pieces[0])
    for cut in pieces[1:]:
        gain = gain * one(*cut)
    return gain


def profile(amount, total, limit, slope):
    loads = [(1 << 20) // math.isqrt(rank ** slope) + 1 for rank in range(2, amount + 1)]
    rest, given = total - limit - (amount - 1), [1] * (amount - 1)
    while rest > 0:
        candidates = [i for i in range(amount - 1) if given[i] < limit]
        pool, left = sum([loads[i] for i in candidates]), rest
        for i in candidates:
            more = min(limit - given[i], max(1, left * loads[i] // pool), rest)
            given[i] = given[i] + more
            rest = rest - more
    return np.array([limit] + given)


def ragged_sizes(own_key, amount, total, reach, lean):
    if amount == 2:
        one = jax.random.randint(own_key, (), max(1, total - reach), min(reach, total - 1) + 1)
        return jnp.stack([one, total - one])
    lengths = jnp.asarray(profile(amount, total, reach, lean), jnp.int32)
    twos = (amount - 1) // 2
    source_of, receiver = lengths[1:1 + 2 * twos:2], lengths[2:2 + 2 * twos:2]
    margin = jnp.minimum(source_of - 1, reach - receiver)
    shifted = jax.random.randint(jax.random.fold_in(own_key, 1), (twos,), 0, 1 << 20) % (margin + 1)
    lengths = lengths.at[1:1 + 2 * twos:2].set(source_of - shifted).at[2:2 + 2 * twos:2].set(receiver + shifted)
    return lengths[jax.random.permutation(jax.random.fold_in(own_key, 2), amount)]


def normal_values(key, extent, width, reach, cuts=(), kind=jnp.bfloat16):
    loudness = shard_levels(key, extent, cuts, -0.22, 0.18) if cuts else 1.0
    result = jax.random.normal(key, extent, jnp.float32) * width * loudness
    return jnp.minimum(jnp.maximum(result, -reach), reach).astype(kind)


def setup_inputs(seed: int = 0) -> dict:
    streams_of = jax.random.split(jax.random.key(seed), 8)
    wave_fields = normal_values(streams_of[0], (NK, R_TOTAL, 2, NB), 1.0, 6.0, ((0, 64), (1, 8)))
    potential_change = normal_values(streams_of[1], (MODES, 2, R_TOTAL), R_TOTAL ** -0.5, 0.046875, ((2, 8),))
    projectors = normal_values(streams_of[2], (4, P_SIZE, R_TOTAL), R_TOTAL ** -0.5, 0.046875, ((2, 8),))
    mode_vectors = normal_values(streams_of[3], (MODES, 3, 2, ATOMS), 1.0, 6.0, (), jnp.float32)
    coupling_base = normal_values(streams_of[4], (P_SIZE, P_SIZE), 0.3, 4.0, (), jnp.float32)
    coupling_change = normal_values(streams_of[5], (MODES, 2, P_SIZE, P_SIZE), 0.3, 4.0, (), jnp.float32)
    projector_atom = jnp.searchsorted(jnp.cumsum(ragged_sizes(streams_of[6], ATOMS, P_SIZE, P_SIZE // 4, 0)), jnp.arange(P_SIZE), side="right").astype(jnp.int32)
    return dict(wave_fields=wave_fields, potential_change=potential_change, projectors=projectors, mode_vectors=mode_vectors, coupling_base=coupling_base, coupling_change=coupling_change, projector_atom=projector_atom)


def weight_waves(own_bands, potential_change):
    wave_real = own_bands[:, 0].astype(jnp.float32)
    wave_imag = own_bands[:, 1].astype(jnp.float32)
    pot_real = potential_change[:, 0].astype(jnp.float32).T
    pot_imag = potential_change[:, 1].astype(jnp.float32).T
    out_real = pot_real[:, :, None] * wave_real[:, None, :] - pot_imag[:, :, None] * wave_imag[:, None, :]
    out_imag = pot_real[:, :, None] * wave_imag[:, None, :] + pot_imag[:, :, None] * wave_real[:, None, :]
    return jnp.stack([out_real, out_imag], axis=1).astype(jnp.bfloat16)


def paired_rows(partner_rows):
    real_part = partner_rows[:, 0]
    imag_part = partner_rows[:, 1]
    return jnp.stack([jnp.stack([real_part, -imag_part], axis=1), jnp.stack([imag_part, real_part], axis=1)], axis=1)


def nonlocal_terms(own_proj, partner_proj, mode_vectors, coupling_base, coupling_change, projector_atom):
    highest = lax.Precision.HIGHEST
    atoms = mode_vectors.shape[-1]
    onehot_atoms = (projector_atom[:, None] == jnp.arange(atoms, dtype=jnp.int32)[None, :]).astype(jnp.float32)
    same_atom = (projector_atom[:, None] == projector_atom[None, :]).astype(jnp.float32)
    base_masked = 0.5 * (coupling_base + coupling_base.T) * same_atom
    change_masked = coupling_change * same_atom
    mode_proj = jnp.einsum("vcxa,ia->vcxi", mode_vectors, onehot_atoms, precision=highest)
    vec_real = mode_proj[:, :, 0]
    vec_imag = mode_proj[:, :, 1]
    own_real = own_proj[0, :, 0]
    own_imag = own_proj[0, :, 1]
    grad_real = own_proj[1:, :, 0]
    grad_imag = own_proj[1:, :, 1]
    part_real = partner_proj[0, :, 0]
    part_imag = partner_proj[0, :, 1]
    pgrad_real = partner_proj[1:, :, 0]
    pgrad_imag = partner_proj[1:, :, 1]

    def contract(left_side, right_side):
        return jnp.einsum("vci,cin->vin", left_side, right_side, precision=highest)

    shift_real = -(contract(vec_real, grad_real) - contract(vec_imag, grad_imag))
    shift_imag = -(contract(vec_real, grad_imag) + contract(vec_imag, grad_real))
    bra_real = -(contract(vec_real, pgrad_real) + contract(vec_imag, pgrad_imag))
    bra_imag = -(contract(vec_imag, pgrad_real) - contract(vec_real, pgrad_imag))
    base_real = jnp.einsum("ij,jn->in", base_masked, own_real, precision=highest)
    base_imag = jnp.einsum("ij,jn->in", base_masked, own_imag, precision=highest)
    first_real = jnp.einsum("vim,in->vmn", bra_real, base_real, precision=highest) - jnp.einsum("vim,in->vmn", bra_imag, base_imag, precision=highest)
    first_imag = jnp.einsum("vim,in->vmn", bra_real, base_imag, precision=highest) + jnp.einsum("vim,in->vmn", bra_imag, base_real, precision=highest)
    change_real = change_masked[:, 0]
    change_imag = change_masked[:, 1]
    inner_real = jnp.einsum("ij,vjn->vin", base_masked, shift_real, precision=highest)
    inner_imag = jnp.einsum("ij,vjn->vin", base_masked, shift_imag, precision=highest)
    inner_real = inner_real + jnp.einsum("vij,jn->vin", change_real, own_real, precision=highest) - jnp.einsum("vij,jn->vin", change_imag, own_imag, precision=highest)
    inner_imag = inner_imag + jnp.einsum("vij,jn->vin", change_real, own_imag, precision=highest) + jnp.einsum("vij,jn->vin", change_imag, own_real, precision=highest)
    tail_real = jnp.einsum("im,vin->vmn", part_real, inner_real, precision=highest) + jnp.einsum("im,vin->vmn", part_imag, inner_imag, precision=highest)
    tail_imag = jnp.einsum("im,vin->vmn", part_real, inner_imag, precision=highest) - jnp.einsum("im,vin->vmn", part_imag, inner_real, precision=highest)
    total = jnp.stack([first_real + tail_real, first_imag + tail_imag], axis=2)
    return jnp.transpose(total, (1, 0, 2, 3))


def reference(wave_fields, potential_change, projectors, mode_vectors, coupling_base, coupling_change, projector_atom):
    grid_points = wave_fields.shape[1]
    bands = wave_fields.shape[3]
    proj_count = projectors.shape[1]
    stacked = projectors.reshape(4 * proj_count, grid_points)

    def per_point(kpoint):
        partner_index = (kpoint + QSTEP) % NK
        own_bands = lax.dynamic_index_in_dim(wave_fields, kpoint, 0, keepdims=False)
        partner = lax.dynamic_index_in_dim(wave_fields, partner_index, 0, keepdims=False)
        own_proj = jnp.dot(stacked, own_bands.reshape(grid_points, 2 * bands), preferred_element_type=jnp.float32).reshape(4, proj_count, 2, bands)
        partner_proj = jnp.dot(stacked, partner.reshape(grid_points, 2 * bands), preferred_element_type=jnp.float32).reshape(4, proj_count, 2, bands)
        weighted = weight_waves(own_bands, potential_change)
        paired = paired_rows(partner)
        local_sum = jnp.einsum("rcom,rcvn->mvon", paired.astype(jnp.float32), weighted.astype(jnp.float32))
        return local_sum + nonlocal_terms(own_proj, partner_proj, mode_vectors, coupling_base, coupling_change, projector_atom)

    return lax.map(per_point, jnp.arange(NK, dtype=jnp.int32))
```

```python
import functools

import jax
import jax.numpy as jnp
from jax import lax
from jax.experimental import pallas as pl
from jax.experimental.pallas import tpu as pltpu
from jax.sharding import PartitionSpec as P

MESH = pl.DeviceIdType.MESH
F32 = jnp.float32
BF16 = jnp.bfloat16
HIGHEST = lax.Precision.HIGHEST
MODES = 4
GROUPS = 4
AHEAD = 3


def dot_nn(left, right, precision=None):
    return jnp.dot(left, right, preferred_element_type=F32, precision=precision)


def dot_nt(left, right, precision=None):
    return lax.dot_general(
        left, right, (((1,), (1,)), ((), ())), preferred_element_type=F32, precision=precision
    )


def nonlocal_rows(rows_ref, all_proj, vec_rows, base_ref, change_ref, same, mixed, result):
    count = same.shape[0]
    rows = rows_ref.shape[1]
    base = 0.5 * (base_ref[...] + base_ref[...].T) * same
    conj_re = rows_ref[0]
    conj_im = -rows_ref[1]

    def group(value, j):
        return value[:, j * count : (j + 1) * count]

    def vec(mode, c):
        at = (mode * 3 + c) * 2
        return vec_rows[at : at + 1, :], vec_rows[at + 1 : at + 2, :]

    bra = []
    for mode in range(MODES):
        total_re = jnp.zeros((rows, count), F32)
        total_im = jnp.zeros((rows, count), F32)
        for c in range(3):
            v_re, v_im = vec(mode, c)
            g_re, g_im = group(conj_re, c + 1), group(conj_im, c + 1)
            total_re = total_re - (v_re * g_re - v_im * g_im)
            total_im = total_im - (v_re * g_im + v_im * g_re)
        bra += [total_re, total_im]
    bra_base = dot_nn(jnp.concatenate(bra, axis=0), base, HIGHEST)
    value = jnp.concatenate([group(conj_re, 0), group(conj_im, 0)], axis=0)
    value_base = dot_nn(value, base, HIGHEST)
    t_re, t_im = value_base[:rows], value_base[rows:]
    for mode in range(MODES):
        with_re = dot_nn(value, change_ref[mode, 0] * same, HIGHEST)
        with_im = dot_nn(value, change_ref[mode, 1] * same, HIGHEST)
        at = mode * 2 * rows
        mixed[at : at + rows, 0:count] = bra_base[at : at + rows] + with_re[:rows] - with_im[rows:]
        mixed[at + rows : at + 2 * rows, 0:count] = (
            bra_base[at + rows : at + 2 * rows] + with_im[:rows] + with_re[rows:]
        )
        for c in range(3):
            v_re, v_im = vec(mode, c)
            lanes = slice((c + 1) * count, (c + 2) * count)
            mixed[at : at + rows, lanes] = -(t_re * v_re - t_im * v_im)
            mixed[at + rows : at + 2 * rows, lanes] = -(t_re * v_im + t_im * v_re)
    by_re = dot_nt(mixed[...], all_proj[0], HIGHEST)
    by_im = dot_nt(mixed[...], all_proj[1], HIGHEST)
    bands = by_re.shape[1]
    for mode in range(MODES):
        at = mode * 2 * rows
        re, im = slice(at, at + rows), slice(at + rows, at + 2 * rows)
        lane = mode * 2 * bands
        result[:, lane : lane + bands] = by_re[re] - by_im[im]
        result[:, lane + bands : lane + 2 * bands] = by_im[re] + by_re[im]


def kernel(
    sizes,
    turned,
    flat,
    pot_rows,
    pot_cols,
    projectors,
    vec_in,
    base_ref,
    change_ref,
    atom_row,
    atom_col,
    out_ref,
    landing,
    weighted,
    weighted_t,
    proj_part,
    proj_land,
    proj_own,
    all_proj,
    rows_land,
    mixed,
    nonlocal_sum,
    sum_send,
    sum_land,
    piece_send,
    piece_land,
    last_rows,
    back_send,
    back_land,
    stream_send,
    stream_recv,
    part_send,
    part_recv,
    all_send,
    all_recv,
    rows_send_sem,
    rows_recv_sem,
    sum_send_sem,
    sum_recv_sem,
    back_send_sem,
    back_recv_sem,
):
    pools, slabs, points, bands = sizes
    rows = bands // slabs
    step = pools // 4
    ka = lax.axis_index("ka")
    ga = lax.axis_index("ga")
    core = lax.rem(ka, 2)
    ahead_k = lax.rem(ka + step, pools)
    behind_k = lax.rem(ka + pools - step, pools)

    barrier = pltpu.get_barrier_semaphore()
    for d in range(1, slabs):
        pl.semaphore_signal(
            barrier, inc=1, device_id=(ka, lax.rem(ga + d, slabs)), device_id_type=MESH
        )
    for other in (ahead_k, behind_k):
        pl.semaphore_signal(barrier, inc=1, device_id=(other, ga), device_id_type=MESH)
    pl.semaphore_wait(barrier, slabs + 1)

    target_k = jnp.where(core == 0, ahead_k, behind_k)
    first_chunk = jnp.where(core == 0, 0, ga + 1)

    def stream(s):
        chunk = lax.rem(first_chunk + s, slabs)
        return pltpu.make_async_remote_copy(
            src_ref=turned.at[chunk],
            dst_ref=landing.at[s],
            send_sem=stream_send.at[s],
            recv_sem=stream_recv.at[s],
            device_id=(target_k, ga),
            device_id_type=MESH,
        )

    for s in range(AHEAD):
        stream(s).start()

    for j in range(slabs):
        proj_part[j] = dot_nt(turned[j], projectors[...])

    def part_copy(d):
        peer = lax.rem(ga + d, slabs)
        return pltpu.make_async_remote_copy(
            src_ref=proj_part.at[peer],
            dst_ref=proj_land.at[d],
            send_sem=part_send.at[d],
            recv_sem=part_recv.at[d],
            device_id=(ka, peer),
            device_id_type=MESH,
        )

    for d in range(1, slabs):
        part_copy(d).start()

    @pl.when(core == 1)
    def _():
        block = 128

        def weigh(i, carry):
            at = pl.ds(pl.multiple_of(i * block, block), block)
            re = flat[at, 0:bands].astype(F32)
            im = flat[at, bands : 2 * bands].astype(F32)
            cols = pot_cols[at, :]
            for mode in range(MODES):
                p_re = cols[:, 2 * mode : 2 * mode + 1]
                p_im = cols[:, 2 * mode + 1 : 2 * mode + 2]
                lane = mode * 2 * bands
                weighted[at, lane : lane + bands] = (p_re * re - p_im * im).astype(BF16)
                weighted[at, lane + bands : lane + 2 * bands] = (p_re * im + p_im * re).astype(BF16)
            return carry

        lax.fori_loop(0, points // block, weigh, 0)

    total = proj_part[ga]
    for d in range(1, slabs):
        part_copy(d).wait_recv()
    for d in range(1, slabs):
        total = total + proj_land[d]
    proj_own[0] = total[:rows]
    proj_own[1] = total[rows:]
    own_rows = pl.ds(pl.multiple_of(ga * rows, rows), rows)
    all_proj[0, own_rows, :] = total[:rows]
    all_proj[1, own_rows, :] = total[rows:]

    def all_copy(d):
        return pltpu.make_async_remote_copy(
            src_ref=proj_own,
            dst_ref=all_proj.at[:, own_rows, :],
            send_sem=all_send.at[d],
            recv_sem=all_recv.at[d],
            device_id=(ka, lax.rem(ga + d, slabs)),
            device_id_type=MESH,
        )

    rows_copy = pltpu.make_async_remote_copy(
        src_ref=proj_own,
        dst_ref=rows_land,
        send_sem=rows_send_sem,
        recv_sem=rows_recv_sem,
        device_id=(behind_k, ga),
        device_id_type=MESH,
    )
    rows_copy.start()
    for d in range(1, slabs):
        all_copy(d).start()

    def all_arrival(d):
        peer = lax.rem(ga + slabs - d, slabs)
        theirs = pl.ds(pl.multiple_of(peer * rows, rows), rows)
        return pltpu.make_async_remote_copy(
            src_ref=proj_own,
            dst_ref=all_proj.at[:, theirs, :],
            send_sem=all_send.at[d],
            recv_sem=all_recv.at[d],
            device_id=(ka, peer),
            device_id_type=MESH,
        )

    def nonlocal_part():
        for d in range(1, slabs):
            all_arrival(d).wait_recv()
        rows_copy.wait_recv()
        atoms = vec_in.shape[1]
        onehot = (
            lax.broadcasted_iota(jnp.int32, (atoms, atom_row.shape[1]), 0) == atom_row[...]
        ).astype(F32)
        vec_rows = dot_nn(vec_in[...], onehot, HIGHEST)
        same = (atom_col[...] == atom_row[...]).astype(F32)
        nonlocal_rows(
            rows_land, all_proj, vec_rows, base_ref, change_ref, same, mixed, nonlocal_sum
        )

    def next_chunk(s):
        stream(s).wait_recv()
        stream(s).wait_send()

        @pl.when(s + AHEAD < slabs)
        def _():
            stream(s + AHEAD).start()

    @pl.when(core == 1)
    def _():
        def rows_copy_to(s):
            return pltpu.make_async_remote_copy(
                src_ref=sum_send.at[s],
                dst_ref=sum_land.at[s],
                send_sem=sum_send_sem.at[s, 0],
                recv_sem=sum_recv_sem.at[s, 0],
                device_id=(ka, lax.rem(ga + 1 + s, slabs)),
                device_id_type=MESH,
            )

        def chunk_sum(s, put):
            for mode in range(MODES):
                lane = mode * 2 * bands
                both = dot_nn(landing[s], weighted[:, lane : lane + 2 * bands])
                put(lane, both[:rows, :bands] + both[rows:, bands:])
                put(lane + bands, both[:rows, bands:] - both[rows:, :bands])

        def one(s, carry):
            next_chunk(s)

            def put(lane, value):
                sum_send[s, :, lane : lane + bands] = value.astype(BF16)

            chunk_sum(s, put)
            rows_copy_to(s).start()
            return carry

        lax.fori_loop(0, 3, one, 0)
        nonlocal_part()
        lax.fori_loop(3, slabs - 1, one, 0)
        next_chunk(slabs - 1)

        def put_last(lane, value):
            last_rows[:, lane : lane + bands] = value + nonlocal_sum[:, lane : lane + bands]

        chunk_sum(slabs - 1, put_last)
        for s in range(slabs - 1):
            rows_copy_to(s).wait_recv()
        for lane in range(0, 2 * MODES * bands, bands):
            value = last_rows[:, lane : lane + bands]
            for s in range(slabs - 1):
                value = value + sum_land[s, :, lane : lane + bands].astype(F32)
            out_ref[:, lane : lane + bands] = value
        for s in range(slabs - 1):
            rows_copy_to(s).wait_send()

    @pl.when(core == 0)
    def _():
        def piece_copy(s, d):
            peer = lax.rem(ga + d, slabs)
            return pltpu.make_async_remote_copy(
                src_ref=piece_send.at[s, pl.ds(pl.multiple_of(peer * rows, rows), rows)],
                dst_ref=piece_land.at[s, pl.ds(d * rows, rows)],
                send_sem=sum_send_sem.at[s, d],
                recv_sem=sum_recv_sem.at[s, d],
                device_id=(ka, peer),
                device_id_type=MESH,
            )

        def back_copy(s):
            return pltpu.make_async_remote_copy(
                src_ref=back_send.at[s],
                dst_ref=back_land.at[s],
                send_sem=back_send_sem.at[s],
                recv_sem=back_recv_sem.at[s],
                device_id=(behind_k, ga),
                device_id_type=MESH,
            )

        def chunk_sum(s):
            block = 512
            for at in range(0, points, block):
                re = landing[s, 0:rows, at : at + block].astype(F32)
                im = landing[s, rows : 2 * rows, at : at + block].astype(F32)
                for mode in range(MODES):
                    p_re = pot_rows[2 * mode : 2 * mode + 1, at : at + block]
                    p_im = pot_rows[2 * mode + 1 : 2 * mode + 2, at : at + block]
                    top = mode * rows
                    weighted_t[top : top + rows, at : at + block] = (p_re * re - p_im * im).astype(
                        BF16
                    )
                    top = (MODES + mode) * rows
                    weighted_t[top : top + rows, at : at + block] = (p_re * im + p_im * re).astype(
                        BF16
                    )
            both = dot_nn(weighted_t[...], flat[...])
            half = MODES * rows
            real = both[:half, :bands] + both[half:, bands:]
            imag = both[half:, :bands] - both[:half, bands:]
            piece_send[s, :, 0:half] = real.T.astype(BF16)
            piece_send[s, :, half : 2 * half] = imag.T.astype(BF16)
            for d in range(1, slabs):
                piece_copy(s, d).start()

        def reduce(s):
            value = piece_send[s, own_rows].astype(F32)
            for d in range(1, slabs):
                piece_copy(s, d).wait_recv()
            for d in range(1, slabs):
                value = value + piece_land[s, d * rows : (d + 1) * rows].astype(F32)
            back_send[s] = value.astype(BF16)
            back_copy(s).start()

        def one(s, carry):
            next_chunk(s)
            chunk_sum(s)

            @pl.when(s > 0)
            def _():
                reduce(s - 1)

            return carry

        lax.fori_loop(0, 3, one, 0)
        nonlocal_part()
        lax.fori_loop(3, slabs, one, 0)
        reduce(slabs - 1)
        for s in range(slabs):
            back_copy(s).wait_recv()
        width = 128
        per = width // rows
        at_lane = lax.broadcasted_iota(jnp.int32, (rows, width), 1)
        for mode in range(MODES):
            for part in range(2):
                for q in range(bands // width):
                    value = jnp.zeros((rows, width), F32)
                    for t in range(per):
                        piece = back_land[q * per + t, :, part * width : (part + 1) * width].astype(
                            F32
                        )
                        shift = (t - mode) * rows % width
                        if shift:
                            piece = pltpu.roll(piece, shift, 1)
                        inside = (at_lane >= t * rows) & (at_lane < (t + 1) * rows)
                        value = jnp.where(inside, piece, value)
                    lane = (mode * 2 + part) * bands + q * width
                    out_ref[:, lane : lane + width] = value + nonlocal_sum[:, lane : lane + width]
        for s in range(slabs):
            back_copy(s).wait_send()
            for d in range(1, slabs):
                piece_copy(s, d).wait_send()

    for d in range(1, slabs):
        part_copy(d).wait_send()
        all_copy(d).wait_send()
    rows_copy.wait_send()


def body(
    wave_fields,
    potential_change,
    projectors,
    mode_vectors,
    coupling_base,
    coupling_change,
    projector_atom,
):
    own = wave_fields[0]
    points, _, bands = own.shape
    pools, slabs = lax.axis_size("ka"), lax.axis_size("ga")
    count = projectors.shape[1]
    atoms = mode_vectors.shape[-1]
    rows = bands // slabs
    turned = jnp.transpose(own.reshape(points, 2, slabs, rows), (2, 1, 3, 0))
    turned = turned.reshape(slabs, 2 * rows, points)
    flat = own.reshape(points, 2 * bands)
    pot_rows = potential_change.reshape(2 * MODES, points).astype(F32)
    wide = 2 * MODES * bands
    vmem = pl.BlockSpec(memory_space=pltpu.VMEM)
    dma = pltpu.SemaphoreType.DMA
    result = pl.pallas_call(
        functools.partial(kernel, (pools, slabs, points, bands)),
        out_shape=jax.ShapeDtypeStruct((rows, wide), F32),
        in_specs=[vmem] * 10,
        out_specs=vmem,
        scratch_shapes=[
            pltpu.VMEM((slabs, 2 * rows, points), BF16),
            pltpu.VMEM((points, wide), BF16),
            pltpu.VMEM((2 * MODES * rows, points), BF16),
            pltpu.VMEM((slabs, 2 * rows, GROUPS * count), F32),
            pltpu.VMEM((slabs, 2 * rows, GROUPS * count), F32),
            pltpu.VMEM((2, rows, GROUPS * count), F32),
            pltpu.VMEM((2, bands, GROUPS * count), F32),
            pltpu.VMEM((2, rows, GROUPS * count), F32),
            pltpu.VMEM((2 * MODES * rows, GROUPS * count), F32),
            pltpu.VMEM((rows, wide), F32),
            pltpu.VMEM((slabs, rows, wide), BF16),
            pltpu.VMEM((slabs, rows, wide), BF16),
            pltpu.VMEM((slabs, bands, 2 * MODES * rows), BF16),
            pltpu.VMEM((slabs, bands, 2 * MODES * rows), BF16),
            pltpu.VMEM((rows, wide), F32),
            pltpu.VMEM((slabs, rows, 2 * MODES * rows), BF16),
            pltpu.VMEM((slabs, rows, 2 * MODES * rows), BF16),
            dma((slabs,)),
            dma((slabs,)),
            dma((slabs,)),
            dma((slabs,)),
            dma((slabs,)),
            dma((slabs,)),
            dma,
            dma,
            dma((slabs, slabs)),
            dma((slabs, slabs)),
            dma((slabs,)),
            dma((slabs,)),
        ],
        compiler_params=pltpu.CompilerParams(
            collective_id=0, has_side_effects=True, vmem_limit_bytes=58 << 20
        ),
        name="matrix_elements",
    )(
        turned,
        flat,
        pot_rows,
        pot_rows.T,
        projectors.reshape(GROUPS * count, points),
        mode_vectors.reshape(MODES * 6, atoms),
        coupling_base,
        coupling_change,
        projector_atom.reshape(1, count),
        projector_atom.reshape(count, 1),
    )
    return result.reshape(1, rows, MODES, 2, bands)


def solution(mesh):
    placed = (
        P("ka", "ga", None, None),
        P(None, None, "ga"),
        P(None, None, "ga"),
        P(),
        P(),
        P(),
        P(),
    )
    return jax.shard_map(
        body, mesh=mesh, in_specs=placed, out_specs=P("ka", "ga", None, None, None), check_vma=False
    )
```

```python
import functools

import jax
import jax.numpy as jnp
from jax import lax
from jax.experimental import pallas as pl
from jax.experimental.pallas import tpu as pltpu
from jax.sharding import PartitionSpec as P

MESH = pl.DeviceIdType.MESH
F32 = jnp.float32
BF16 = jnp.bfloat16
HIGHEST = lax.Precision.HIGHEST
MODES = 4
GROUPS = 4
AHEAD = 3
WIDTH = 128


def dot_nn(left, right, precision=None):
    return jnp.dot(left, right, preferred_element_type=F32, precision=precision)


def dot_nt(left, right, precision=None):
    return lax.dot_general(
        left, right, (((1,), (1,)), ((), ())), preferred_element_type=F32, precision=precision
    )


def nonlocal_rows(rows_ref, all_proj, vec_rows, base_ref, change_ref, same, mixed, result):
    count = same.shape[0]
    rows = rows_ref.shape[1]
    base = 0.5 * (base_ref[...] + base_ref[...].T) * same
    conj_re = rows_ref[0]
    conj_im = -rows_ref[1]

    def group(value, j):
        return value[:, j * count : (j + 1) * count]

    def vec(mode, c):
        at = (mode * 3 + c) * 2
        return vec_rows[at : at + 1, :], vec_rows[at + 1 : at + 2, :]

    bra = []
    for mode in range(MODES):
        total_re = jnp.zeros((rows, count), F32)
        total_im = jnp.zeros((rows, count), F32)
        for c in range(3):
            v_re, v_im = vec(mode, c)
            g_re, g_im = group(conj_re, c + 1), group(conj_im, c + 1)
            total_re = total_re - (v_re * g_re - v_im * g_im)
            total_im = total_im - (v_re * g_im + v_im * g_re)
        bra += [total_re, total_im]
    bra_base = dot_nn(jnp.concatenate(bra, axis=0), base, HIGHEST)
    value = jnp.concatenate([group(conj_re, 0), group(conj_im, 0)], axis=0)
    value_base = dot_nn(value, base, HIGHEST)
    t_re, t_im = value_base[:rows], value_base[rows:]
    for mode in range(MODES):
        with_re = dot_nn(value, change_ref[mode, 0] * same, HIGHEST)
        with_im = dot_nn(value, change_ref[mode, 1] * same, HIGHEST)
        at = mode * 2 * rows
        mixed[at : at + rows, 0:count] = bra_base[at : at + rows] + with_re[:rows] - with_im[rows:]
        mixed[at + rows : at + 2 * rows, 0:count] = (
            bra_base[at + rows : at + 2 * rows] + with_im[:rows] + with_re[rows:]
        )
        for c in range(3):
            v_re, v_im = vec(mode, c)
            lanes = slice((c + 1) * count, (c + 2) * count)
            mixed[at : at + rows, lanes] = -(t_re * v_re - t_im * v_im)
            mixed[at + rows : at + 2 * rows, lanes] = -(t_re * v_im + t_im * v_re)
    by_re = dot_nt(mixed[...], all_proj[0], HIGHEST)
    by_im = dot_nt(mixed[...], all_proj[1], HIGHEST)
    bands = by_re.shape[1]
    for mode in range(MODES):
        at = mode * 2 * rows
        re, im = slice(at, at + rows), slice(at + rows, at + 2 * rows)
        lane = mode * 2 * bands
        result[:, lane : lane + bands] = by_re[re] - by_im[im]
        result[:, lane + bands : lane + 2 * bands] = by_im[re] + by_re[im]


def kernel(
    sizes,
    wave_in,
    pot_in,
    projectors_in,
    vec_in,
    base_in,
    change_in,
    atom_in,
    out_ref,
    raw,
    pot_raw,
    projectors,
    vec_ref,
    base_ref,
    change_ref,
    atom_row,
    pick,
    pot_rows,
    turned,
    flat,
    landing,
    weighted,
    weighted_t,
    proj_part,
    proj_x,
    proj_send,
    proj_y,
    proj_own,
    all_proj,
    rows_land,
    mixed,
    nonlocal_sum,
    sum_send,
    sum_land,
    held,
    pair_send,
    pair_land,
    piece_send,
    piece_land,
    piece_held,
    half_send,
    half_land,
    back_send,
    back_land,
    last_send,
    last_land,
    stream_sems,
    proj_x_sems,
    gather_sems,
    lone_sems,
    sum_sems,
    piece_sems,
    half_sems,
    back_sems,
    local_sems,
):
    pools, slabs, points, bands = sizes
    rows = bands // slabs
    across = slabs // 2
    step = pools // 4
    ka = lax.axis_index("ka")
    ga = lax.axis_index("ga")
    core = lax.rem(ka, 2)
    x = ga // 2
    half = lax.rem(ga, 2)
    ahead_k = lax.rem(ka + step, pools)
    behind_k = lax.rem(ka + pools - step, pools)

    def x_peer(d):
        return lax.rem(x + d, across)

    def at_x(d):
        return (ka, x_peer(d) * 2 + half)

    other = x * 2 + 1 - half
    other_half = (ka, other)

    def remote(src, dst, sems, where):
        return pltpu.make_async_remote_copy(
            src_ref=src,
            dst_ref=dst,
            send_sem=sems[0],
            recv_sem=sems[1],
            device_id=where,
            device_id_type=MESH,
        )

    def rows_of(first, count):
        return pl.ds(pl.multiple_of(first, count), count)

    barrier = pltpu.get_barrier_semaphore()
    peers = [at_x(d) for d in range(1, across)] + [other_half]
    peers += [(k, g) for k in (ahead_k, behind_k) for g in (ga, other)]
    for where in peers:
        pl.semaphore_signal(barrier, inc=1, device_id=where, device_id_type=MESH)

    first_half = jnp.where(core == 0, 0, x_peer(1) // 2)

    def fetch_wave(h):
        lanes = pl.ds(pl.multiple_of(h * WIDTH, WIDTH), WIDTH)
        return pltpu.make_async_copy(wave_in.at[:, :, lanes], raw.at[h], local_sems.at[h])

    fetches = [
        pltpu.make_async_copy(src, dst, local_sems.at[2 + i])
        for i, (src, dst) in enumerate(
            (
                (pot_in, pot_raw),
                (projectors_in, projectors),
                (vec_in, vec_ref),
                (base_in, base_ref),
                (change_in, change_ref),
                (atom_in, atom_row),
            )
        )
    ]
    fetch_wave(first_half).start()
    fetch_wave(1 - first_half).start()
    for fetch in fetches:
        fetch.start()
    row = lax.broadcasted_iota(jnp.int32, pick.shape, 0)
    column = lax.broadcasted_iota(jnp.int32, pick.shape, 1)
    part = (row >= WIDTH).astype(jnp.int32)
    pick[...] = (column == 2 * (row - WIDTH * part) + part).astype(BF16)
    paired = raw.reshape(2, 2 * points, WIDTH)

    def turn(h):
        fetch_wave(h).wait()
        chunks = WIDTH // rows

        def block(b, carry):
            here = rows_of(b * WIDTH, WIDTH)
            planes = dot_nn(pick[...], paired[h, rows_of(b * 2 * WIDTH, 2 * WIDTH), :]).astype(BF16)
            for c in range(2):
                plane = planes[c * WIDTH : (c + 1) * WIDTH]
                flat[here, pl.ds(pl.multiple_of(c * bands + h * WIDTH, WIDTH), WIDTH)] = plane
                across_points = plane.T
                for j in range(chunks):
                    turned[h * chunks + j, c * rows : (c + 1) * rows, here] = across_points[
                        j * rows : (j + 1) * rows
                    ]
            return carry

        lax.fori_loop(0, points // WIDTH, block, 0, unroll=4)

    turn(first_half)
    pl.semaphore_wait(barrier, len(peers))

    target_k = jnp.where(core == 0, ahead_k, behind_k)

    def stream(s):
        place = lax.rem(x + 1 + lax.rem(s, across), across) * 2
        side = jnp.where(s < across, 1 - half, half)
        chunk = jnp.where(core == 0, s, place + side)
        return remote(
            turned.at[chunk],
            landing.at[s],
            (stream_sems.at[0, s], stream_sems.at[1, s]),
            (target_k, ga),
        )

    stream(0).start()
    turn(1 - first_half)
    for s in range(1, AHEAD):
        stream(s).start()
    for fetch in fetches:
        fetch.wait()

    turned_rows = turned.reshape(slabs * 2 * rows, points)
    proj_part[...] = dot_nt(turned_rows[...], projectors[...]).reshape(proj_part.shape)

    def proj_x_copy(d):
        return remote(
            proj_part.at[pl.ds(x_peer(d) * 2, 2)],
            proj_x.at[d - 1],
            (proj_x_sems.at[0, d], proj_x_sems.at[1, d]),
            at_x(d),
        )

    for d in range(1, across):
        proj_x_copy(d).start()

    for mode in range(MODES):
        pot_rows[2 * mode : 2 * mode + 2, :] = pot_raw[mode].astype(F32)

    @pl.when(core == 1)
    def _():
        block = 128

        def weigh(i, carry):
            at = pl.ds(pl.multiple_of(i * block, block), block)
            re = flat[at, 0:bands].astype(F32)
            im = flat[at, bands : 2 * bands].astype(F32)
            cols = pot_rows[:, at].T
            for mode in range(MODES):
                p_re = cols[:, 2 * mode : 2 * mode + 1]
                p_im = cols[:, 2 * mode + 1 : 2 * mode + 2]
                lane = mode * 2 * bands
                weighted[at, lane : lane + bands] = (p_re * re - p_im * im).astype(BF16)
                weighted[at, lane + bands : lane + 2 * bands] = (p_re * im + p_im * re).astype(BF16)
            return carry

        lax.fori_loop(0, points // block, weigh, 0)

    proj_y_copy = remote(proj_send, proj_y, (lone_sems.at[0], lone_sems.at[1]), other_half)
    own_rows = rows_of(ga * rows, rows)
    pair_rows = rows_of(x * 2 * rows, 2 * rows)
    gather_y = remote(
        proj_own,
        all_proj.at[:, own_rows, :],
        (lone_sems.at[2], lone_sems.at[3]),
        other_half,
    )
    gather_y_arrival = remote(
        proj_own,
        all_proj.at[:, rows_of((x * 2 + 1 - half) * rows, rows), :],
        (lone_sems.at[2], lone_sems.at[3]),
        other_half,
    )
    rows_copy = remote(
        proj_own, rows_land, (lone_sems.at[4], lone_sems.at[5]), (behind_k, ga)
    )

    def gather_x(d, first):
        block = rows_of(first * 2 * rows, 2 * rows)
        return remote(
            all_proj.at[:, block, :],
            all_proj.at[:, block, :],
            (gather_sems.at[0, d], gather_sems.at[1, d]),
            at_x(d),
        )

    def proj_sum(side):
        value = proj_part[x * 2 + side]
        for d in range(1, across):
            value = value + proj_x[d - 1, side]
        return value

    def proj_stage_0():
        for d in range(1, across):
            proj_x_copy(d).wait_recv()
        proj_send[...] = proj_sum(1 - half)
        proj_y_copy.start()

    def proj_stage_1():
        proj_y_copy.wait_recv()
        value = proj_sum(half) + proj_y[...]
        proj_own[0] = value[:rows]
        proj_own[1] = value[rows:]
        rows_copy.start()
        gather_y.start()
        all_proj[0, own_rows, :] = value[:rows]
        all_proj[1, own_rows, :] = value[rows:]

    def proj_stage_2():
        gather_y_arrival.wait_recv()
        for d in range(1, across):
            gather_x(d, x).start()

    def nonlocal_part():
        for d in range(1, across):
            gather_x(d, x_peer(across - d)).wait_recv()
        rows_copy.wait_recv()
        atoms = vec_ref.shape[1]
        onehot = (
            lax.broadcasted_iota(jnp.int32, (atoms, atom_row.shape[1]), 0) == atom_row[...]
        ).astype(F32)
        vec_rows = dot_nn(vec_ref[...], onehot, HIGHEST)
        same = dot_nn(onehot.T, onehot)
        nonlocal_rows(
            rows_land, all_proj, vec_rows, base_ref, change_ref, same, mixed, nonlocal_sum
        )

    def next_chunk(s):
        stream(s).wait_recv()
        stream(s).wait_send()

        @pl.when(s + AHEAD < slabs)
        def _():
            stream(s + AHEAD).start()

    def beside(s):
        for at, stage in enumerate((proj_stage_1, proj_stage_2, None, nonlocal_part)):
            if stage is not None:
                pl.when(s == at)(stage)

    proj_stage_0()

    @pl.when(core == 1)
    def _():
        def sum_copy(s):
            return remote(
                sum_send.at[s],
                sum_land.at[s],
                (sum_sems.at[0, s], sum_sems.at[1, s]),
                at_x(1 + lax.rem(s, across)),
            )

        pair_copy = remote(pair_send, pair_land, (lone_sems.at[6], lone_sems.at[7]), other_half)

        def chunk_sum(s, put):
            for mode in range(MODES):
                lane = mode * 2 * bands
                both = dot_nn(landing[s], weighted[:, lane : lane + 2 * bands])
                put(lane, both[:rows, :bands] + both[rows:, bands:])
                put(lane + bands, both[:rows, bands:] - both[rows:, :bands])

        def arrived(first, lane):
            value = held[:, lane : lane + bands]
            for s in range(first, first + across - 1):
                value = value + sum_land[s, :, lane : lane + bands].astype(F32)
            return value

        def one(s, carry):
            next_chunk(s)
            kept = lax.rem(s, across) == across - 1

            def put_send(lane, value):
                sum_send[s, :, lane : lane + bands] = value.astype(BF16)

            def put_held(lane, value):
                held[:, lane : lane + bands] = value

            @pl.when(kept)
            def _():
                chunk_sum(s, put_held)

            @pl.when(jnp.logical_not(kept))
            def _():
                chunk_sum(s, put_send)
                sum_copy(s).start()

            @pl.when(s == across)
            def _():
                for i in range(across - 1):
                    sum_copy(i).wait_recv()
                for lane in range(0, 2 * MODES * bands, bands):
                    pair_send[:, lane : lane + bands] = arrived(0, lane).astype(BF16)
                pair_copy.start()

            beside(s)
            return carry

        lax.fori_loop(0, slabs, one, 0)
        pair_copy.wait_recv()
        for i in range(across, slabs - 1):
            sum_copy(i).wait_recv()
        for i in range(2 * MODES):
            here = slice(i * bands, (i + 1) * bands)
            out_ref[:, i // 2, i % 2, :] = (
                arrived(across, i * bands) + pair_land[:, here].astype(F32) + nonlocal_sum[:, here]
            )
        for s in list(range(across - 1)) + list(range(across, slabs - 1)):
            sum_copy(s).wait_send()
        pair_copy.wait_send()

    @pl.when(core == 0)
    def _():
        def piece_copy(s, d):
            return remote(
                piece_send.at[s, rows_of(x_peer(d) * 2 * rows, 2 * rows)],
                piece_land.at[s, pl.ds((d - 1) * 2 * rows, 2 * rows)],
                (piece_sems.at[0, s, d], piece_sems.at[1, s, d]),
                at_x(d),
            )

        def half_copy(s):
            return remote(
                half_send.at[s],
                half_land.at[s],
                (half_sems.at[0, s], half_sems.at[1, s]),
                other_half,
            )

        def back_copy(s):
            return remote(
                back_send.at[s],
                back_land.at[s],
                (back_sems.at[0, s], back_sems.at[1, s]),
                (behind_k, ga),
            )

        def last_copy(side):
            return remote(
                last_send.at[side],
                last_land.at[side],
                (lone_sems.at[8 + 2 * side], lone_sems.at[9 + 2 * side]),
                (behind_k, ga if side == 0 else other),
            )

        def chunk_sum(s):
            block = 512
            for at in range(0, points, block):
                re = landing[s, 0:rows, at : at + block].astype(F32)
                im = landing[s, rows : 2 * rows, at : at + block].astype(F32)
                for mode in range(MODES):
                    p_re = pot_rows[2 * mode : 2 * mode + 1, at : at + block]
                    p_im = pot_rows[2 * mode + 1 : 2 * mode + 2, at : at + block]
                    top = mode * rows
                    weighted_t[top : top + rows, at : at + block] = (p_re * re - p_im * im).astype(
                        BF16
                    )
                    top = (MODES + mode) * rows
                    weighted_t[top : top + rows, at : at + block] = (p_re * im + p_im * re).astype(
                        BF16
                    )
            both = dot_nn(weighted_t[...], flat[...])
            many = MODES * rows
            real = both[:many, :bands] + both[many:, bands:]
            imag = both[many:, :bands] - both[:many, bands:]
            piece_send[s, :, 0:many] = real.T.astype(BF16)
            piece_send[s, :, many : 2 * many] = imag.T.astype(BF16)
            for d in range(1, across):
                piece_copy(s, d).start()

        def total(s, side):
            first = pl.multiple_of((x * 2 + side) * rows, rows)
            value = piece_send[s, pl.ds(first, rows)].astype(F32)
            for d in range(1, across):
                first = pl.multiple_of(((d - 1) * 2 + side) * rows, rows)
                value = value + piece_land[s, pl.ds(first, rows)].astype(F32)
            return value

        def reduce_x(s):
            for d in range(1, across):
                piece_copy(s, d).wait_recv()
            half_send[s] = total(s, 1 - half).astype(BF16)
            half_copy(s).start()
            piece_held[s] = total(s, half)

        def reduce_y(s):
            half_copy(s).wait_recv()
            back_send[s] = (piece_held[s] + half_land[s].astype(F32)).astype(BF16)
            back_copy(s).start()

        def one(s, carry):
            next_chunk(s)
            chunk_sum(s)

            @pl.when(s >= 1)
            def _():
                reduce_x(s - 1)

            @pl.when(s >= 2)
            def _():
                reduce_y(s - 2)

            beside(s)
            return carry

        lax.fori_loop(0, slabs, one, 0)
        for d in range(1, across):
            piece_copy(slabs - 1, d).wait_recv()
        for side in range(2):
            last_send[side] = total(slabs - 1, half if side == 0 else 1 - half).astype(BF16)
            last_copy(side).start()
        reduce_y(slabs - 2)
        for s in range(slabs - 1):
            back_copy(s).wait_recv()
        for side in range(2):
            last_copy(side).wait_recv()
        per = WIDTH // rows
        at_lane = lax.broadcasted_iota(jnp.int32, (rows, WIDTH), 1)

        def summed(chunk, part):
            here = slice(part * WIDTH, (part + 1) * WIDTH)
            if chunk < slabs - 1:
                return back_land[chunk, :, here].astype(F32)
            return last_land[0, :, here].astype(F32) + last_land[1, :, here].astype(F32)

        for mode in range(MODES):
            for part in range(2):
                for q in range(bands // WIDTH):
                    value = jnp.zeros((rows, WIDTH), F32)
                    for t in range(per):
                        piece = summed(q * per + t, part)
                        shift = (t - mode) * rows % WIDTH
                        if shift:
                            piece = pltpu.roll(piece, shift, 1)
                        inside = (at_lane >= t * rows) & (at_lane < (t + 1) * rows)
                        value = jnp.where(inside, piece, value)
                    lane = (mode * 2 + part) * bands + q * WIDTH
                    out_ref[:, mode, part, q * WIDTH : (q + 1) * WIDTH] = (
                        value + nonlocal_sum[:, lane : lane + WIDTH]
                    )
        for s in range(slabs):
            if s < slabs - 1:
                back_copy(s).wait_send()
                half_copy(s).wait_send()
            else:
                last_copy(0).wait_send()
                last_copy(1).wait_send()
            for d in range(1, across):
                piece_copy(s, d).wait_send()

    for d in range(1, across):
        proj_x_copy(d).wait_send()
        gather_x(d, x).wait_send()
    proj_y_copy.wait_send()
    gather_y.wait_send()
    rows_copy.wait_send()


def body(
    wave_fields,
    potential_change,
    projectors,
    mode_vectors,
    coupling_base,
    coupling_change,
    projector_atom,
):
    own = wave_fields[0]
    points, _, bands = own.shape
    pools, slabs = lax.axis_size("ka"), lax.axis_size("ga")
    count = projectors.shape[1]
    atoms = mode_vectors.shape[-1]
    rows = bands // slabs
    across = slabs // 2
    columns = GROUPS * count
    wide = 2 * MODES * bands
    part_wide = 2 * MODES * rows
    vmem = pl.BlockSpec(memory_space=pltpu.VMEM)
    dma = pltpu.SemaphoreType.DMA
    result = pl.pallas_call(
        functools.partial(kernel, (pools, slabs, points, bands)),
        out_shape=jax.ShapeDtypeStruct((rows, MODES, 2, bands), F32),
        in_specs=[pl.BlockSpec(memory_space=pl.ANY)] * 7,
        out_specs=vmem,
        scratch_shapes=[
            pltpu.VMEM((bands // WIDTH, points, 2, WIDTH), BF16),
            pltpu.VMEM(potential_change.shape, BF16),
            pltpu.VMEM((columns, points), BF16),
            pltpu.VMEM((MODES * 6, atoms), F32),
            pltpu.VMEM(coupling_base.shape, F32),
            pltpu.VMEM(coupling_change.shape, F32),
            pltpu.VMEM((1, count), jnp.int32),
            pltpu.VMEM((2 * WIDTH, 2 * WIDTH), BF16),
            pltpu.VMEM((2 * MODES, points), F32),
            pltpu.VMEM((slabs, 2 * rows, points), BF16),
            pltpu.VMEM((points, 2 * bands), BF16),
            pltpu.VMEM((slabs, 2 * rows, points), BF16),
            pltpu.VMEM((points, wide), BF16),
            pltpu.VMEM((2 * MODES * rows, points), BF16),
            pltpu.VMEM((slabs, 2 * rows, columns), F32),
            pltpu.VMEM((across - 1, 2, 2 * rows, columns), F32),
            pltpu.VMEM((2 * rows, columns), F32),
            pltpu.VMEM((2 * rows, columns), F32),
            pltpu.VMEM((2, rows, columns), F32),
            pltpu.VMEM((2, bands, columns), F32),
            pltpu.VMEM((2, rows, columns), F32),
            pltpu.VMEM((2 * MODES * rows, columns), F32),
            pltpu.VMEM((rows, wide), F32),
            pltpu.VMEM((slabs, rows, wide), BF16),
            pltpu.VMEM((slabs, rows, wide), BF16),
            pltpu.VMEM((rows, wide), F32),
            pltpu.VMEM((rows, wide), BF16),
            pltpu.VMEM((rows, wide), BF16),
            pltpu.VMEM((slabs, bands, part_wide), BF16),
            pltpu.VMEM((slabs, (across - 1) * 2 * rows, part_wide), BF16),
            pltpu.VMEM((slabs, rows, part_wide), F32),
            pltpu.VMEM((slabs, rows, part_wide), BF16),
            pltpu.VMEM((slabs, rows, part_wide), BF16),
            pltpu.VMEM((slabs, rows, part_wide), BF16),
            pltpu.VMEM((slabs, rows, part_wide), BF16),
            pltpu.VMEM((2, rows, part_wide), BF16),
            pltpu.VMEM((2, rows, part_wide), BF16),
            dma((2, slabs)),
            dma((2, across)),
            dma((2, across)),
            dma((12,)),
            dma((2, slabs)),
            dma((2, slabs, across)),
            dma((2, slabs)),
            dma((2, slabs)),
            dma((8,)),
        ],
        compiler_params=pltpu.CompilerParams(
            collective_id=0, has_side_effects=True, vmem_limit_bytes=58 << 20
        ),
        name="matrix_elements",
    )(
        own,
        potential_change,
        projectors.reshape(columns, points),
        mode_vectors.reshape(MODES * 6, atoms),
        coupling_base,
        coupling_change,
        projector_atom.reshape(1, count),
    )
    return result[None]


def solution(mesh):
    placed = (
        P("ka", "ga", None, None),
        P(None, None, "ga"),
        P(None, None, "ga"),
        P(),
        P(),
        P(),
        P(),
    )
    return jax.shard_map(
        body, mesh=mesh, in_specs=placed, out_specs=P("ka", "ga", None, None, None), check_vma=False
    )
```

```python
import functools

import jax
import jax.numpy as jnp
from jax import lax
from jax.experimental import pallas as pl
from jax.experimental.pallas import tpu as pltpu
from jax.sharding import PartitionSpec as P

MESH = pl.DeviceIdType.MESH
F32 = jnp.float32
BF16 = jnp.bfloat16
HIGHEST = lax.Precision.HIGHEST
MODES = 4
GROUPS = 4
AHEAD = 3
SLACK = 1
QUARTERS = 4
WIDTH = 128
STAGES = (1, 2, 3, 5)
LAG_X, LAG_Y = 1, 3
DIRECT = 2


def dot_nn(left, right, precision=None):
    return jnp.dot(left, right, preferred_element_type=F32, precision=precision)


def dot_nt(left, right, precision=None):
    return lax.dot_general(
        left, right, (((1,), (1,)), ((), ())), preferred_element_type=F32, precision=precision
    )


def nonlocal_rows(rows_ref, all_proj, vec_rows, base_ref, change_ref, same, mixed, result):
    count = same.shape[0]
    rows = rows_ref.shape[1]
    base = 0.5 * (base_ref[...] + base_ref[...].T) * same
    conj_re = rows_ref[0]
    conj_im = -rows_ref[1]

    def group(value, j):
        return value[:, j * count : (j + 1) * count]

    def vec(mode, c):
        at = (mode * 3 + c) * 2
        return vec_rows[at : at + 1, :], vec_rows[at + 1 : at + 2, :]

    bra = []
    for mode in range(MODES):
        total_re = jnp.zeros((rows, count), F32)
        total_im = jnp.zeros((rows, count), F32)
        for c in range(3):
            v_re, v_im = vec(mode, c)
            g_re, g_im = group(conj_re, c + 1), group(conj_im, c + 1)
            total_re = total_re - (v_re * g_re - v_im * g_im)
            total_im = total_im - (v_re * g_im + v_im * g_re)
        bra += [total_re, total_im]
    bra_base = dot_nn(jnp.concatenate(bra, axis=0), base, HIGHEST)
    value = jnp.concatenate([group(conj_re, 0), group(conj_im, 0)], axis=0)
    value_base = dot_nn(value, base, HIGHEST)
    t_re, t_im = value_base[:rows], value_base[rows:]
    for mode in range(MODES):
        with_re = dot_nn(value, change_ref[mode, 0] * same, HIGHEST)
        with_im = dot_nn(value, change_ref[mode, 1] * same, HIGHEST)
        at = mode * 2 * rows
        mixed[at : at + rows, 0:count] = bra_base[at : at + rows] + with_re[:rows] - with_im[rows:]
        mixed[at + rows : at + 2 * rows, 0:count] = (
            bra_base[at + rows : at + 2 * rows] + with_im[:rows] + with_re[rows:]
        )
        for c in range(3):
            v_re, v_im = vec(mode, c)
            lanes = slice((c + 1) * count, (c + 2) * count)
            mixed[at : at + rows, lanes] = -(t_re * v_re - t_im * v_im)
            mixed[at + rows : at + 2 * rows, lanes] = -(t_re * v_im + t_im * v_re)
    by_re = dot_nt(mixed[...], all_proj[0], HIGHEST)
    by_im = dot_nt(mixed[...], all_proj[1], HIGHEST)
    bands = by_re.shape[1]
    for mode in range(MODES):
        at = mode * 2 * rows
        re, im = slice(at, at + rows), slice(at + rows, at + 2 * rows)
        lane = mode * 2 * bands
        result[:, lane : lane + bands] = by_re[re] - by_im[im]
        result[:, lane + bands : lane + 2 * bands] = by_im[re] + by_re[im]


def kernel(
    sizes,
    wave_in,
    pot_in,
    projectors_in,
    vec_in,
    base_in,
    change_in,
    atom_in,
    out_ref,
    raw,
    pot_raw,
    projectors,
    vec_ref,
    base_ref,
    change_ref,
    atom_row,
    pick,
    pot_rows,
    turned,
    flat,
    landing,
    weighted,
    weighted_t,
    proj_part,
    proj_x,
    proj_send,
    proj_y,
    proj_own,
    all_proj,
    rows_land,
    mixed,
    nonlocal_sum,
    sum_send,
    sum_land,
    held,
    pair_send,
    pair_land,
    piece_send,
    piece_land,
    piece_held,
    half_send,
    half_land,
    back_send,
    back_land,
    last_send,
    last_land,
    home_land,
    sums,
    sums_t,
    stream_sems,
    proj_x_sems,
    gather_sems,
    lone_sems,
    sum_sems,
    piece_sems,
    half_sems,
    back_sems,
    last_sems,
    home_sems,
    local_sems,
    raw_sems,
    paces,
):
    pools, slabs, points, bands = sizes
    rows = bands // slabs
    across = slabs // 2
    step = pools // 4
    ka = lax.axis_index("ka")
    ga = lax.axis_index("ga")
    core = lax.rem(ka, 2)
    x = ga // 2
    half = lax.rem(ga, 2)
    ahead_k = lax.rem(ka + step, pools)
    behind_k = lax.rem(ka + pools - step, pools)

    def x_peer(d):
        return lax.rem(x + d, across)

    def at_x(d):
        return (ka, x_peer(d) * 2 + half)

    other = x * 2 + 1 - half
    other_half = (ka, other)

    def remote(src, dst, sems, where):
        return pltpu.make_async_remote_copy(
            src_ref=src,
            dst_ref=dst,
            send_sem=sems[0],
            recv_sem=sems[1],
            device_id=where,
            device_id_type=MESH,
        )

    def rows_of(first, count):
        return pl.ds(pl.multiple_of(first, count), count)

    barrier = pltpu.get_barrier_semaphore()
    peers = [at_x(d) for d in range(1, across)] + [other_half]
    peers += [(k, lax.rem(ga + d, slabs)) for k in (ahead_k, behind_k) for d in range(slabs)]
    between = [(lax.rem(ka + d, pools), ga) for d in (step // 2, pools - step // 2)]
    peers += between
    for where in peers:
        pl.semaphore_signal(barrier, inc=1, device_id=where, device_id_type=MESH)

    first_half = jnp.where(core == 0, 0, x_peer(1) // 2)

    quarter = points // QUARTERS

    def fetch_wave(h, q):
        lanes = pl.ds(pl.multiple_of(h * WIDTH, WIDTH), WIDTH)
        here = pl.ds(q * quarter, quarter)
        return pltpu.make_async_copy(
            wave_in.at[here, :, lanes], raw.at[h, here], raw_sems.at[h, q]
        )

    fetches = [
        pltpu.make_async_copy(src, dst, local_sems.at[i])
        for i, (src, dst) in enumerate(
            (
                (pot_in, pot_raw),
                (projectors_in, projectors),
                (vec_in, vec_ref),
                (base_in, base_ref),
                (change_in, change_ref),
                (atom_in, atom_row),
            )
        )
    ]
    for h in (first_half, 1 - first_half):
        for q in range(QUARTERS):
            fetch_wave(h, q).start()
    for fetch in fetches:
        fetch.start()
    row = lax.broadcasted_iota(jnp.int32, pick.shape, 0)
    column = lax.broadcasted_iota(jnp.int32, pick.shape, 1)
    part = (row >= WIDTH).astype(jnp.int32)
    pick[...] = (column == 2 * (row - WIDTH * part) + part).astype(BF16)
    paired = raw.reshape(2, 2 * points, WIDTH)

    def turn(h, q):
        fetch_wave(h, q).wait()
        chunks = WIDTH // rows

        def block(b, carry):
            here = rows_of(b * WIDTH, WIDTH)
            planes = dot_nn(pick[...], paired[h, rows_of(b * 2 * WIDTH, 2 * WIDTH), :]).astype(BF16)
            for c in range(2):
                plane = planes[c * WIDTH : (c + 1) * WIDTH]
                flat[here, pl.ds(pl.multiple_of(c * bands + h * WIDTH, WIDTH), WIDTH)] = plane
                across_points = plane.T
                for j in range(chunks):
                    turned[h * chunks + j, c * rows : (c + 1) * rows, here] = across_points[
                        j * rows : (j + 1) * rows
                    ]
            return carry

        blocks = quarter // WIDTH
        lax.fori_loop(q * blocks, (q + 1) * blocks, block, 0, unroll=True)

    turn(first_half, 0)
    pl.semaphore_wait(barrier, len(peers))

    target_k = jnp.where(core == 0, ahead_k, behind_k)

    final = slabs - 1
    quarters = [pl.ds(q * quarter, quarter) for q in range(QUARTERS)]

    def stream(s, points_here=slice(None), sem=None):
        place = lax.rem(x + 1 + lax.rem(s, across), across) * 2
        side = jnp.where(s < across, 1 - half, half)
        chunk = jnp.where(core == 0, s, place + side)
        sem = s if sem is None else sem
        return remote(
            turned.at[chunk, :, points_here],
            landing.at[s, :, points_here],
            (stream_sems.at[0, sem], stream_sems.at[1, sem]),
            (target_k, ga),
        )

    def last_quarter(q):
        return stream(final, quarters[q], final + q)

    for q, here in enumerate(quarters):
        if q:
            turn(first_half, q)
        stream(0, here).start()
    for q in range(QUARTERS):
        turn(1 - first_half, q)
    for s in range(1, AHEAD):
        stream(s).start()
    for fetch in fetches:
        fetch.wait()

    turned_rows = turned.reshape(slabs * 2 * rows, points)
    proj_part[...] = dot_nt(turned_rows[...], projectors[...]).reshape(proj_part.shape)

    def proj_x_copy(d):
        return remote(
            proj_part.at[pl.ds(x_peer(d) * 2, 2)],
            proj_x.at[d - 1],
            (proj_x_sems.at[0, d], proj_x_sems.at[1, d]),
            at_x(d),
        )

    for d in range(1, across):
        proj_x_copy(d).start()

    for mode in range(MODES):
        pot_rows[2 * mode : 2 * mode + 2, :] = pot_raw[mode].astype(F32)

    @pl.when(core == 1)
    def _():
        block = 128

        def weigh(i, carry):
            at = pl.ds(pl.multiple_of(i * block, block), block)
            re = flat[at, 0:bands].astype(F32)
            im = flat[at, bands : 2 * bands].astype(F32)
            cols = pot_rows[:, at].T
            for mode in range(MODES):
                p_re = cols[:, 2 * mode : 2 * mode + 1]
                p_im = cols[:, 2 * mode + 1 : 2 * mode + 2]
                lane = mode * 2 * bands
                weighted[at, lane : lane + bands] = (p_re * re - p_im * im).astype(BF16)
                weighted[at, lane + bands : lane + 2 * bands] = (p_re * im + p_im * re).astype(BF16)
            return carry

        lax.fori_loop(0, points // block, weigh, 0)

    proj_y_copy = remote(proj_send, proj_y, (lone_sems.at[0], lone_sems.at[1]), other_half)
    own_rows = rows_of(ga * rows, rows)
    pair_rows = rows_of(x * 2 * rows, 2 * rows)
    gather_y = remote(
        proj_own,
        all_proj.at[:, own_rows, :],
        (lone_sems.at[2], lone_sems.at[3]),
        other_half,
    )
    gather_y_arrival = remote(
        proj_own,
        all_proj.at[:, rows_of((x * 2 + 1 - half) * rows, rows), :],
        (lone_sems.at[2], lone_sems.at[3]),
        other_half,
    )
    rows_copy = remote(
        proj_own, rows_land, (lone_sems.at[4], lone_sems.at[5]), (behind_k, ga)
    )

    def gather_x(d, first):
        block = rows_of(first * 2 * rows, 2 * rows)
        return remote(
            all_proj.at[:, block, :],
            all_proj.at[:, block, :],
            (gather_sems.at[0, d], gather_sems.at[1, d]),
            at_x(d),
        )

    def proj_sum(side):
        value = proj_part[x * 2 + side]
        for d in range(1, across):
            value = value + proj_x[d - 1, side]
        return value

    def proj_stage_0():
        for d in range(1, across):
            proj_x_copy(d).wait_recv()
        proj_send[...] = proj_sum(1 - half)
        proj_y_copy.start()

    def proj_stage_1():
        proj_y_copy.wait_recv()
        value = proj_sum(half) + proj_y[...]
        proj_own[0] = value[:rows]
        proj_own[1] = value[rows:]
        rows_copy.start()
        gather_y.start()
        all_proj[0, own_rows, :] = value[:rows]
        all_proj[1, own_rows, :] = value[rows:]

    def proj_stage_2():
        gather_y_arrival.wait_recv()
        for d in range(1, across):
            gather_x(d, x).start()

    def nonlocal_part():
        for d in range(1, across):
            gather_x(d, x_peer(across - d)).wait_recv()
        rows_copy.wait_recv()
        atoms = vec_ref.shape[1]
        onehot = (
            lax.broadcasted_iota(jnp.int32, (atoms, atom_row.shape[1]), 0) == atom_row[...]
        ).astype(F32)
        vec_rows = dot_nn(vec_ref[...], onehot, HIGHEST)
        same = dot_nn(onehot.T, onehot)
        nonlocal_rows(
            rows_land, all_proj, vec_rows, base_ref, change_ref, same, mixed, nonlocal_sum
        )

    def next_chunk(s):
        stream(s).wait_recv()
        for i, where in enumerate(between):
            pl.semaphore_signal(paces.at[i], inc=1, device_id=where, device_id_type=MESH)
        stream(s).wait_send()

        @pl.when(jnp.logical_and(s + AHEAD <= final, s >= SLACK))
        def _():
            for i in range(2):
                pl.semaphore_wait(paces.at[i], 1)

        @pl.when(s + AHEAD < final)
        def _():
            stream(s + AHEAD).start()

        @pl.when(s + AHEAD == final)
        def _():
            for q in range(QUARTERS):
                last_quarter(q).start()

    def beside(s):
        stages = (proj_stage_0, proj_stage_1, proj_stage_2, nonlocal_part)
        for at, stage in zip(STAGES, stages):
            pl.when(s == at)(stage)

    @pl.when(core == 1)
    def _():
        def sum_copy(s):
            return remote(
                sum_send.at[s],
                sum_land.at[s],
                (sum_sems.at[0, s], sum_sems.at[1, s]),
                at_x(1 + lax.rem(s, across)),
            )

        pair_copy = remote(pair_send, pair_land, (lone_sems.at[6], lone_sems.at[7]), other_half)

        def parts_of(both, lane, put):
            put(lane, both[:rows, :bands] + both[rows:, bands:])
            put(lane + bands, both[:rows, bands:] - both[rows:, :bands])

        def chunk_sum(s, put):
            for lane in range(0, 2 * MODES * bands, 2 * bands):
                both = dot_nn(landing[s], weighted[:, lane : lane + 2 * bands])
                parts_of(both, lane, put)

        def arrived(first, lane):
            value = held[:, lane : lane + bands]
            for s in range(first, first + across - 1):
                value = value + sum_land[s, :, lane : lane + bands].astype(F32)
            return value

        def put_held(lane, value):
            held[:, lane : lane + bands] = value

        def one(s, carry):
            next_chunk(s)
            kept = s == across - 1

            def put_send(lane, value):
                sum_send[s, :, lane : lane + bands] = value.astype(BF16)

            @pl.when(kept)
            def _():
                chunk_sum(s, put_held)

            @pl.when(jnp.logical_not(kept))
            def _():
                chunk_sum(s, put_send)
                sum_copy(s).start()

            @pl.when(s == across)
            def _():
                for i in range(across - 1):
                    sum_copy(i).wait_recv()
                for lane in range(0, 2 * MODES * bands, bands):
                    pair_send[:, lane : lane + bands] = arrived(0, lane).astype(BF16)
                pair_copy.start()

            beside(s)
            return carry

        lax.fori_loop(0, final, one, 0)
        for q, here in enumerate(quarters):
            last_quarter(q).wait_recv()
            for lane in range(0, 2 * MODES * bands, 2 * bands):
                lanes = slice(lane, lane + 2 * bands)
                both = dot_nn(landing[final, :, here], weighted[here, lanes])
                both = both if q == 0 else sums[:, lanes] + both
                if q < QUARTERS - 1:
                    sums[:, lanes] = both
                else:
                    parts_of(both, lane, put_held)
        pair_copy.wait_recv()
        for i in range(across, slabs - 1):
            sum_copy(i).wait_recv()
        for i in range(2 * MODES):
            here = slice(i * bands, (i + 1) * bands)
            out_ref[:, i // 2, i % 2, :] = (
                arrived(across, i * bands) + pair_land[:, here].astype(F32) + nonlocal_sum[:, here]
            )
        for s in list(range(across - 1)) + list(range(across, slabs - 1)):
            sum_copy(s).wait_send()
        pair_copy.wait_send()

    @pl.when(core == 0)
    def _():
        def piece_copy(s, d):
            return remote(
                piece_send.at[s, rows_of(x_peer(d) * 2 * rows, 2 * rows)],
                piece_land.at[s, pl.ds((d - 1) * 2 * rows, 2 * rows)],
                (piece_sems.at[0, s, d], piece_sems.at[1, s, d]),
                at_x(d),
            )

        def half_copy(s):
            return remote(
                half_send.at[s],
                half_land.at[s],
                (half_sems.at[0, s], half_sems.at[1, s]),
                other_half,
            )

        def back_copy(s):
            return remote(
                back_send.at[s],
                back_land.at[s],
                (back_sems.at[0, s], back_sems.at[1, s]),
                (behind_k, ga),
            )

        passed = final - DIRECT

        def last_copy(i, side):
            return remote(
                last_send.at[i, side],
                last_land.at[i, side],
                (last_sems.at[0, i, side], last_sems.at[1, i, side]),
                (behind_k, ga if side == 0 else other),
            )

        def home_copy(d):
            peer = lax.rem(ga + d, slabs)
            return remote(
                piece_send.at[final, rows_of(peer * rows, rows)],
                home_land.at[d],
                (home_sems.at[0, d], home_sems.at[1, d]),
                (behind_k, peer),
            )

        many = MODES * rows

        def weigh_turned(s, here):
            re = landing[s, 0:rows, here].astype(F32)
            im = landing[s, rows : 2 * rows, here].astype(F32)
            for mode in range(MODES):
                p_re = pot_rows[2 * mode : 2 * mode + 1, here]
                p_im = pot_rows[2 * mode + 1 : 2 * mode + 2, here]
                top = mode * rows
                weighted_t[top : top + rows, here] = (p_re * re - p_im * im).astype(BF16)
                top = many + mode * rows
                weighted_t[top : top + rows, here] = (p_re * im + p_im * re).astype(BF16)

        def pieces(s, both):
            real = both[:many, :bands] + both[many:, bands:]
            imag = both[many:, :bands] - both[:many, bands:]
            piece_send[s, :, 0:many] = real.T.astype(BF16)
            piece_send[s, :, many : 2 * many] = imag.T.astype(BF16)

        def total(s, side):
            first = pl.multiple_of((x * 2 + side) * rows, rows)
            value = piece_send[s, pl.ds(first, rows)].astype(F32)
            for d in range(1, across):
                first = pl.multiple_of(((d - 1) * 2 + side) * rows, rows)
                value = value + piece_land[s, pl.ds(first, rows)].astype(F32)
            return value

        def reduce_x(s):
            for d in range(1, across):
                piece_copy(s, d).wait_recv()

            @pl.when(s < passed)
            def _():
                half_send[s] = total(s, 1 - half).astype(BF16)
                half_copy(s).start()
                piece_held[s] = total(s, half)

            @pl.when(s >= passed)
            def _():
                for side in range(2):
                    last_send[s - passed, side] = total(s, half if side == 0 else 1 - half).astype(
                        BF16
                    )
                    last_copy(s - passed, side).start()

        def reduce_y(s):
            half_copy(s).wait_recv()
            back_send[s] = (piece_held[s] + half_land[s].astype(F32)).astype(BF16)
            back_copy(s).start()

        def one(s, carry):
            next_chunk(s)
            for here in quarters:
                weigh_turned(s, here)
            pieces(s, dot_nn(weighted_t[...], flat[...]))
            for d in range(1, across):
                piece_copy(s, d).start()

            @pl.when(s >= LAG_X)
            def _():
                reduce_x(s - LAG_X)

            @pl.when(jnp.logical_and(s >= LAG_Y, s < passed + LAG_Y))
            def _():
                reduce_y(s - LAG_Y)

            beside(s)
            return carry

        lax.fori_loop(0, final, one, 0)
        for q, here in enumerate(quarters):
            last_quarter(q).wait_recv()
            weigh_turned(final, here)
            both = dot_nn(weighted_t[:, here], flat[here, :])
            both = both if q == 0 else sums_t[...] + both
            if q < QUARTERS - 1:
                sums_t[...] = both
            else:
                pieces(final, both)
            if q == QUARTERS - 2:
                for s in range(final - LAG_X, final):
                    reduce_x(s)
                for s in range(final - LAG_Y, passed):
                    reduce_y(s)
        for d in range(slabs):
            home_copy(d).start()
        for s in range(passed):
            back_copy(s).wait_recv()
        for i in range(DIRECT):
            for side in range(2):
                last_copy(i, side).wait_recv()
        for d in range(slabs):
            home_copy(d).wait_recv()
        per = WIDTH // rows
        at_lane = lax.broadcasted_iota(jnp.int32, (rows, WIDTH), 1)

        def summed(chunk, part):
            here = slice(part * WIDTH, (part + 1) * WIDTH)
            if chunk < passed:
                return back_land[chunk, :, here].astype(F32)
            if chunk < final:
                both = [last_land[chunk - passed, side, :, here] for side in range(2)]
            else:
                both = [home_land[d, :, here] for d in range(slabs)]
            return sum(piece.astype(F32) for piece in both)

        for mode in range(MODES):
            for part in range(2):
                for q in range(bands // WIDTH):
                    value = jnp.zeros((rows, WIDTH), F32)
                    for t in range(per):
                        piece = summed(q * per + t, part)
                        shift = (t - mode) * rows % WIDTH
                        if shift:
                            piece = pltpu.roll(piece, shift, 1)
                        inside = (at_lane >= t * rows) & (at_lane < (t + 1) * rows)
                        value = jnp.where(inside, piece, value)
                    lane = (mode * 2 + part) * bands + q * WIDTH
                    out_ref[:, mode, part, q * WIDTH : (q + 1) * WIDTH] = (
                        value + nonlocal_sum[:, lane : lane + WIDTH]
                    )
        for s in range(slabs):
            if s < passed:
                back_copy(s).wait_send()
                half_copy(s).wait_send()
            elif s < final:
                last_copy(s - passed, 0).wait_send()
                last_copy(s - passed, 1).wait_send()
            for d in range(slabs):
                if s == final:
                    home_copy(d).wait_send()
                elif 0 < d < across:
                    piece_copy(s, d).wait_send()

    for q in range(QUARTERS):
        last_quarter(q).wait_send()
    for i in range(2):
        pl.semaphore_wait(paces.at[i], AHEAD - 1 + SLACK)
    for d in range(1, across):
        proj_x_copy(d).wait_send()
        gather_x(d, x).wait_send()
    proj_y_copy.wait_send()
    gather_y.wait_send()
    rows_copy.wait_send()


def body(
    wave_fields,
    potential_change,
    projectors,
    mode_vectors,
    coupling_base,
    coupling_change,
    projector_atom,
):
    own = wave_fields[0]
    points, _, bands = own.shape
    pools, slabs = lax.axis_size("ka"), lax.axis_size("ga")
    count = projectors.shape[1]
    atoms = mode_vectors.shape[-1]
    rows = bands // slabs
    across = slabs // 2
    columns = GROUPS * count
    wide = 2 * MODES * bands
    part_wide = 2 * MODES * rows
    vmem = pl.BlockSpec(memory_space=pltpu.VMEM)
    dma = pltpu.SemaphoreType.DMA
    result = pl.pallas_call(
        functools.partial(kernel, (pools, slabs, points, bands)),
        out_shape=jax.ShapeDtypeStruct((rows, MODES, 2, bands), F32),
        in_specs=[pl.BlockSpec(memory_space=pl.ANY)] * 7,
        out_specs=vmem,
        scratch_shapes=[
            pltpu.VMEM((bands // WIDTH, points, 2, WIDTH), BF16),
            pltpu.VMEM(potential_change.shape, BF16),
            pltpu.VMEM((columns, points), BF16),
            pltpu.VMEM((MODES * 6, atoms), F32),
            pltpu.VMEM(coupling_base.shape, F32),
            pltpu.VMEM(coupling_change.shape, F32),
            pltpu.VMEM((1, count), jnp.int32),
            pltpu.VMEM((2 * WIDTH, 2 * WIDTH), BF16),
            pltpu.VMEM((2 * MODES, points), F32),
            pltpu.VMEM((slabs, 2 * rows, points), BF16),
            pltpu.VMEM((points, 2 * bands), BF16),
            pltpu.VMEM((slabs, 2 * rows, points), BF16),
            pltpu.VMEM((points, wide), BF16),
            pltpu.VMEM((2 * MODES * rows, points), BF16),
            pltpu.VMEM((slabs, 2 * rows, columns), F32),
            pltpu.VMEM((across - 1, 2, 2 * rows, columns), F32),
            pltpu.VMEM((2 * rows, columns), F32),
            pltpu.VMEM((2 * rows, columns), F32),
            pltpu.VMEM((2, rows, columns), F32),
            pltpu.VMEM((2, bands, columns), F32),
            pltpu.VMEM((2, rows, columns), F32),
            pltpu.VMEM((2 * MODES * rows, columns), F32),
            pltpu.VMEM((rows, wide), F32),
            pltpu.VMEM((slabs, rows, wide), BF16),
            pltpu.VMEM((slabs, rows, wide), BF16),
            pltpu.VMEM((rows, wide), F32),
            pltpu.VMEM((rows, wide), BF16),
            pltpu.VMEM((rows, wide), BF16),
            pltpu.VMEM((slabs, bands, part_wide), BF16),
            pltpu.VMEM((slabs, (across - 1) * 2 * rows, part_wide), BF16),
            pltpu.VMEM((slabs, rows, part_wide), F32),
            pltpu.VMEM((slabs, rows, part_wide), BF16),
            pltpu.VMEM((slabs, rows, part_wide), BF16),
            pltpu.VMEM((slabs, rows, part_wide), BF16),
            pltpu.VMEM((slabs, rows, part_wide), BF16),
            pltpu.VMEM((DIRECT, 2, rows, part_wide), BF16),
            pltpu.VMEM((DIRECT, 2, rows, part_wide), BF16),
            pltpu.VMEM((slabs, rows, part_wide), BF16),
            pltpu.VMEM((2 * rows, wide), F32),
            pltpu.VMEM((part_wide, 2 * bands), F32),
            dma((2, slabs - 1 + QUARTERS)),
            dma((2, across)),
            dma((2, across)),
            dma((8,)),
            dma((2, slabs)),
            dma((2, slabs, across)),
            dma((2, slabs)),
            dma((2, slabs)),
            dma((2, DIRECT, 2)),
            dma((2, slabs)),
            dma((6,)),
            dma((2, QUARTERS)),
            pltpu.SemaphoreType.REGULAR((2,)),
        ],
        compiler_params=pltpu.CompilerParams(
            collective_id=0, has_side_effects=True, vmem_limit_bytes=58 << 20
        ),
        name="matrix_elements",
    )(
        own,
        potential_change,
        projectors.reshape(columns, points),
        mode_vectors.reshape(MODES * 6, atoms),
        coupling_base,
        coupling_change,
        projector_atom.reshape(1, count),
    )
    return result[None]


def solution(mesh):
    placed = (
        P("ka", "ga", None, None),
        P(None, None, "ga"),
        P(None, None, "ga"),
        P(),
        P(),
        P(),
        P(),
    )
    return jax.shard_map(
        body, mesh=mesh, in_specs=placed, out_specs=P("ka", "ga", None, None, None), check_vma=False
    )
```

```python
import functools

import jax
import jax.numpy as jnp
from jax import lax
from jax.experimental import pallas as pl
from jax.experimental.pallas import tpu as pltpu
from jax.sharding import PartitionSpec as P

MESH = pl.DeviceIdType.MESH
F32 = jnp.float32
BF16 = jnp.bfloat16
HIGHEST = lax.Precision.HIGHEST
MODES = 4
GROUPS = 4
AHEAD = 3
SLACK = 1
QUARTERS = 4
WIDTH = 128
STAGES = (1, 2, 3, 5)
LAG_X, LAG_Y = 1, 3
DIRECT = 2


def dot_nn(left, right, precision=None):
    return jnp.dot(left, right, preferred_element_type=F32, precision=precision)


def dot_nt(left, right, precision=None):
    return lax.dot_general(
        left, right, (((1,), (1,)), ((), ())), preferred_element_type=F32, precision=precision
    )


def nonlocal_rows(rows_ref, all_proj, vec_rows, base_ref, change_ref, same, mixed, result):
    count = same.shape[0]
    rows = rows_ref.shape[1]
    base = 0.5 * (base_ref[...] + base_ref[...].T) * same
    conj_re = rows_ref[0]
    conj_im = -rows_ref[1]

    def group(value, j):
        return value[:, j * count : (j + 1) * count]

    def vec(mode, c):
        at = (mode * 3 + c) * 2
        return vec_rows[at : at + 1, :], vec_rows[at + 1 : at + 2, :]

    bra = []
    for mode in range(MODES):
        total_re = jnp.zeros((rows, count), F32)
        total_im = jnp.zeros((rows, count), F32)
        for c in range(3):
            v_re, v_im = vec(mode, c)
            g_re, g_im = group(conj_re, c + 1), group(conj_im, c + 1)
            total_re = total_re - (v_re * g_re - v_im * g_im)
            total_im = total_im - (v_re * g_im + v_im * g_re)
        bra += [total_re, total_im]
    bra_base = dot_nn(jnp.concatenate(bra, axis=0), base, HIGHEST)
    value = jnp.concatenate([group(conj_re, 0), group(conj_im, 0)], axis=0)
    value_base = dot_nn(value, base, HIGHEST)
    t_re, t_im = value_base[:rows], value_base[rows:]
    for mode in range(MODES):
        with_re = dot_nn(value, change_ref[mode, 0] * same, HIGHEST)
        with_im = dot_nn(value, change_ref[mode, 1] * same, HIGHEST)
        at = mode * 2 * rows
        mixed[at : at + rows, 0:count] = bra_base[at : at + rows] + with_re[:rows] - with_im[rows:]
        mixed[at + rows : at + 2 * rows, 0:count] = (
            bra_base[at + rows : at + 2 * rows] + with_im[:rows] + with_re[rows:]
        )
        for c in range(3):
            v_re, v_im = vec(mode, c)
            lanes = slice((c + 1) * count, (c + 2) * count)
            mixed[at : at + rows, lanes] = -(t_re * v_re - t_im * v_im)
            mixed[at + rows : at + 2 * rows, lanes] = -(t_re * v_im + t_im * v_re)
    by_re = dot_nt(mixed[...], all_proj[0], HIGHEST)
    by_im = dot_nt(mixed[...], all_proj[1], HIGHEST)
    bands = by_re.shape[1]
    for mode in range(MODES):
        at = mode * 2 * rows
        re, im = slice(at, at + rows), slice(at + rows, at + 2 * rows)
        lane = mode * 2 * bands
        result[:, lane : lane + bands] = by_re[re] - by_im[im]
        result[:, lane + bands : lane + 2 * bands] = by_im[re] + by_re[im]


def kernel(
    sizes,
    wave_in,
    pot_in,
    projectors_in,
    vec_in,
    base_in,
    change_in,
    atom_in,
    out_ref,
    raw,
    pot_raw,
    projectors,
    vec_ref,
    base_ref,
    change_ref,
    atom_row,
    pick,
    pot_rows,
    turned,
    flat,
    landing,
    weighted,
    weighted_t,
    proj_part,
    proj_x,
    proj_send,
    proj_y,
    proj_own,
    all_proj,
    rows_land,
    mixed,
    nonlocal_sum,
    sum_send,
    sum_land,
    held,
    pair_send,
    pair_land,
    piece_send,
    piece_land,
    piece_held,
    half_send,
    half_land,
    back_send,
    back_land,
    last_send,
    last_land,
    home_land,
    sums,
    sums_t,
    stream_sems,
    proj_x_sems,
    gather_sems,
    lone_sems,
    sum_sems,
    piece_sems,
    half_sems,
    back_sems,
    last_sems,
    home_sems,
    local_sems,
    raw_sems,
    paces,
):
    pools, slabs, points, bands = sizes
    rows = bands // slabs
    across = slabs // 2
    step = pools // 4
    ka = lax.axis_index("ka")
    ga = lax.axis_index("ga")
    core = lax.rem(ka, 2)
    x = ga // 2
    half = lax.rem(ga, 2)
    ahead_k = lax.rem(ka + step, pools)
    behind_k = lax.rem(ka + pools - step, pools)

    def x_peer(d):
        return lax.rem(x + d, across)

    def at_x(d):
        return (ka, x_peer(d) * 2 + half)

    other = x * 2 + 1 - half
    other_half = (ka, other)

    def remote(src, dst, sems, where):
        return pltpu.make_async_remote_copy(
            src_ref=src,
            dst_ref=dst,
            send_sem=sems[0],
            recv_sem=sems[1],
            device_id=where,
            device_id_type=MESH,
        )

    def rows_of(first, count):
        return pl.ds(pl.multiple_of(first, count), count)

    barrier = pltpu.get_barrier_semaphore()
    peers = [at_x(d) for d in range(1, across)] + [other_half]
    peers += [(k, lax.rem(ga + d, slabs)) for k in (ahead_k, behind_k) for d in range(slabs)]
    between = [(lax.rem(ka + d, pools), ga) for d in (step // 2, pools - step // 2)]
    peers += between
    for where in peers:
        pl.semaphore_signal(barrier, inc=1, device_id=where, device_id_type=MESH)

    first_half = jnp.where(core == 0, 0, x_peer(1) // 2)

    quarter = points // QUARTERS

    def fetch_wave(h, q):
        lanes = pl.ds(pl.multiple_of(h * WIDTH, WIDTH), WIDTH)
        here = pl.ds(q * quarter, quarter)
        return pltpu.make_async_copy(
            wave_in.at[here, :, lanes], raw.at[h, here], raw_sems.at[h, q]
        )

    fetches = [
        pltpu.make_async_copy(src, dst, local_sems.at[i])
        for i, (src, dst) in enumerate(
            (
                (pot_in, pot_raw),
                (projectors_in, projectors),
                (vec_in, vec_ref),
                (base_in, base_ref),
                (change_in, change_ref),
                (atom_in, atom_row),
            )
        )
    ]
    for h in (first_half, 1 - first_half):
        for q in range(QUARTERS):
            fetch_wave(h, q).start()
    for fetch in fetches:
        fetch.start()
    row = lax.broadcasted_iota(jnp.int32, pick.shape, 0)
    column = lax.broadcasted_iota(jnp.int32, pick.shape, 1)
    part = (row >= WIDTH).astype(jnp.int32)
    pick[...] = (column == 2 * (row - WIDTH * part) + part).astype(BF16)
    paired = raw.reshape(2, 2 * points, WIDTH)

    def turn(h, q):
        fetch_wave(h, q).wait()
        chunks = WIDTH // rows

        def block(b, carry):
            here = rows_of(b * WIDTH, WIDTH)
            planes = dot_nn(pick[...], paired[h, rows_of(b * 2 * WIDTH, 2 * WIDTH), :]).astype(BF16)
            for c in range(2):
                plane = planes[c * WIDTH : (c + 1) * WIDTH]
                flat[here, pl.ds(pl.multiple_of(c * bands + h * WIDTH, WIDTH), WIDTH)] = plane
                across_points = plane.T
                for j in range(chunks):
                    turned[h * chunks + j, c * rows : (c + 1) * rows, here] = across_points[
                        j * rows : (j + 1) * rows
                    ]
            return carry

        blocks = quarter // WIDTH
        lax.fori_loop(q * blocks, (q + 1) * blocks, block, 0, unroll=True)

    turn(first_half, 0)
    pl.semaphore_wait(barrier, len(peers))

    target_k = jnp.where(core == 0, ahead_k, behind_k)

    final = slabs - 1
    quarters = [pl.ds(q * quarter, quarter) for q in range(QUARTERS)]

    def stream(s, points_here=slice(None), sem=None):
        place = lax.rem(x + 1 + lax.rem(s, across), across) * 2
        side = jnp.where(s < across, 1 - half, half)
        chunk = jnp.where(core == 0, s, place + side)
        sem = s if sem is None else sem
        return remote(
            turned.at[chunk, :, points_here],
            landing.at[s, :, points_here],
            (stream_sems.at[0, sem], stream_sems.at[1, sem]),
            (target_k, ga),
        )

    def last_quarter(q):
        return stream(final, quarters[q], final + q)

    for q, here in enumerate(quarters):
        if q:
            turn(first_half, q)
        stream(0, here).start()
    for q in range(QUARTERS):
        turn(1 - first_half, q)
    for s in range(1, AHEAD):
        stream(s).start()
    for fetch in fetches:
        fetch.wait()

    turned_rows = turned.reshape(slabs * 2 * rows, points)
    proj_part[...] = dot_nt(turned_rows[...], projectors[...]).reshape(proj_part.shape)

    def proj_x_copy(d):
        return remote(
            proj_part.at[pl.ds(x_peer(d) * 2, 2)],
            proj_x.at[d - 1],
            (proj_x_sems.at[0, d], proj_x_sems.at[1, d]),
            at_x(d),
        )

    for d in range(1, across):
        proj_x_copy(d).start()

    for mode in range(MODES):
        pot_rows[2 * mode : 2 * mode + 2, :] = pot_raw[mode].astype(F32)

    @pl.when(core == 1)
    def _():
        block = 128

        def weigh(i, carry):
            at = pl.ds(pl.multiple_of(i * block, block), block)
            re = flat[at, 0:bands].astype(F32)
            im = flat[at, bands : 2 * bands].astype(F32)
            cols = pot_rows[:, at].T
            for mode in range(MODES):
                p_re = cols[:, 2 * mode : 2 * mode + 1]
                p_im = cols[:, 2 * mode + 1 : 2 * mode + 2]
                lane = mode * 2 * bands
                weighted[at, lane : lane + bands] = (p_re * re - p_im * im).astype(BF16)
                weighted[at, lane + bands : lane + 2 * bands] = (p_re * im + p_im * re).astype(BF16)
            return carry

        lax.fori_loop(0, points // block, weigh, 0)

    proj_y_copy = remote(proj_send, proj_y, (lone_sems.at[0], lone_sems.at[1]), other_half)
    own_rows = rows_of(ga * rows, rows)
    pair_rows = rows_of(x * 2 * rows, 2 * rows)
    gather_y = remote(
        proj_own,
        all_proj.at[:, own_rows, :],
        (lone_sems.at[2], lone_sems.at[3]),
        other_half,
    )
    gather_y_arrival = remote(
        proj_own,
        all_proj.at[:, rows_of((x * 2 + 1 - half) * rows, rows), :],
        (lone_sems.at[2], lone_sems.at[3]),
        other_half,
    )
    rows_copy = remote(
        proj_own, rows_land, (lone_sems.at[4], lone_sems.at[5]), (behind_k, ga)
    )

    def gather_x(d, first):
        block = rows_of(first * 2 * rows, 2 * rows)
        return remote(
            all_proj.at[:, block, :],
            all_proj.at[:, block, :],
            (gather_sems.at[0, d], gather_sems.at[1, d]),
            at_x(d),
        )

    def proj_sum(side):
        value = proj_part[x * 2 + side]
        for d in range(1, across):
            value = value + proj_x[d - 1, side]
        return value

    def proj_stage_0():
        for d in range(1, across):
            proj_x_copy(d).wait_recv()
        proj_send[...] = proj_sum(1 - half)
        proj_y_copy.start()

    def proj_stage_1():
        proj_y_copy.wait_recv()
        value = proj_sum(half) + proj_y[...]
        proj_own[0] = value[:rows]
        proj_own[1] = value[rows:]
        rows_copy.start()
        gather_y.start()
        all_proj[0, own_rows, :] = value[:rows]
        all_proj[1, own_rows, :] = value[rows:]

    def proj_stage_2():
        gather_y_arrival.wait_recv()
        for d in range(1, across):
            gather_x(d, x).start()

    def nonlocal_part():
        for d in range(1, across):
            gather_x(d, x_peer(across - d)).wait_recv()
        rows_copy.wait_recv()
        atoms = vec_ref.shape[1]
        onehot = (
            lax.broadcasted_iota(jnp.int32, (atoms, atom_row.shape[1]), 0) == atom_row[...]
        ).astype(F32)
        vec_rows = dot_nn(vec_ref[...], onehot, HIGHEST)
        same = dot_nn(onehot.T, onehot)
        nonlocal_rows(
            rows_land, all_proj, vec_rows, base_ref, change_ref, same, mixed, nonlocal_sum
        )

    def next_chunk(s):
        stream(s).wait_recv()
        for i, where in enumerate(between):
            pl.semaphore_signal(paces.at[i], inc=1, device_id=where, device_id_type=MESH)
        stream(s).wait_send()

        @pl.when(jnp.logical_and(s + AHEAD <= final, s >= SLACK))
        def _():
            for i in range(2):
                pl.semaphore_wait(paces.at[i], 1)

        @pl.when(s + AHEAD < final)
        def _():
            stream(s + AHEAD).start()

        @pl.when(s + AHEAD == final)
        def _():
            for q in range(QUARTERS):
                last_quarter(q).start()

    def beside(s):
        stages = (proj_stage_0, proj_stage_1, proj_stage_2, nonlocal_part)
        for at, stage in zip(STAGES, stages):
            pl.when(s == at)(stage)

    @pl.when(core == 1)
    def _():
        def sum_copy(s):
            return remote(
                sum_send.at[s],
                sum_land.at[s],
                (sum_sems.at[0, s], sum_sems.at[1, s]),
                at_x(1 + lax.rem(s, across)),
            )

        pair_copy = remote(pair_send, pair_land, (lone_sems.at[6], lone_sems.at[7]), other_half)

        def parts_of(both, lane, put):
            put(lane, both[:rows, :bands] + both[rows:, bands:])
            put(lane + bands, both[:rows, bands:] - both[rows:, :bands])

        def chunk_sum(s, put):
            for lane in range(0, 2 * MODES * bands, 2 * bands):
                both = dot_nn(landing[s], weighted[:, lane : lane + 2 * bands])
                parts_of(both, lane, put)

        def arrived(first, lane):
            value = held[:, lane : lane + bands]
            for s in range(first, first + across - 1):
                value = value + sum_land[s, :, lane : lane + bands].astype(F32)
            return value

        def put_held(lane, value):
            held[:, lane : lane + bands] = value

        def one(s, carry):
            next_chunk(s)
            kept = s == across - 1

            def put_send(lane, value):
                sum_send[s, :, lane : lane + bands] = value.astype(BF16)

            @pl.when(kept)
            def _():
                chunk_sum(s, put_held)

            @pl.when(jnp.logical_not(kept))
            def _():
                chunk_sum(s, put_send)
                sum_copy(s).start()

            @pl.when(s == across)
            def _():
                for i in range(across - 1):
                    sum_copy(i).wait_recv()
                for lane in range(0, 2 * MODES * bands, bands):
                    pair_send[:, lane : lane + bands] = arrived(0, lane).astype(BF16)
                pair_copy.start()

            beside(s)
            return carry

        lax.fori_loop(0, final, one, 0)
        for q, here in enumerate(quarters):
            last_quarter(q).wait_recv()
            for lane in range(0, 2 * MODES * bands, 2 * bands):
                lanes = slice(lane, lane + 2 * bands)
                both = dot_nn(landing[final, :, here], weighted[here, lanes])
                both = both if q == 0 else sums[:, lanes] + both
                if q < QUARTERS - 1:
                    sums[:, lanes] = both
                else:
                    parts_of(both, lane, put_held)
        pair_copy.wait_recv()
        for i in range(across, slabs - 1):
            sum_copy(i).wait_recv()
        for i in range(2 * MODES):
            here = slice(i * bands, (i + 1) * bands)
            out_ref[:, i // 2, i % 2, :] = (
                arrived(across, i * bands) + pair_land[:, here].astype(F32) + nonlocal_sum[:, here]
            )
        for s in list(range(across - 1)) + list(range(across, slabs - 1)):
            sum_copy(s).wait_send()
        pair_copy.wait_send()

    @pl.when(core == 0)
    def _():
        def piece_copy(s, d):
            return remote(
                piece_send.at[s, rows_of(x_peer(d) * 2 * rows, 2 * rows)],
                piece_land.at[s, pl.ds((d - 1) * 2 * rows, 2 * rows)],
                (piece_sems.at[0, s, d], piece_sems.at[1, s, d]),
                at_x(d),
            )

        def half_copy(s):
            return remote(
                half_send.at[s],
                half_land.at[s],
                (half_sems.at[0, s], half_sems.at[1, s]),
                other_half,
            )

        def back_copy(s):
            return remote(
                back_send.at[s],
                back_land.at[s],
                (back_sems.at[0, s], back_sems.at[1, s]),
                (behind_k, ga),
            )

        passed = final - DIRECT

        def last_copy(i, side):
            return remote(
                last_send.at[i, side],
                last_land.at[i, side],
                (last_sems.at[0, i, side], last_sems.at[1, i, side]),
                (behind_k, ga if side == 0 else other),
            )

        def home_copy(d):
            peer = lax.rem(ga + d, slabs)
            return remote(
                piece_send.at[final, rows_of(peer * rows, rows)],
                home_land.at[d],
                (home_sems.at[0, d], home_sems.at[1, d]),
                (behind_k, peer),
            )

        many = MODES * rows

        def weigh_turned(s, here):
            re = landing[s, 0:rows, here].astype(F32)
            im = landing[s, rows : 2 * rows, here].astype(F32)
            for mode in range(MODES):
                p_re = pot_rows[2 * mode : 2 * mode + 1, here]
                p_im = pot_rows[2 * mode + 1 : 2 * mode + 2, here]
                top = mode * rows
                weighted_t[top : top + rows, here] = (p_re * re - p_im * im).astype(BF16)
                top = many + mode * rows
                weighted_t[top : top + rows, here] = (p_re * im + p_im * re).astype(BF16)

        def pieces(s, both):
            real = both[:many, :bands] + both[many:, bands:]
            imag = both[many:, :bands] - both[:many, bands:]
            piece_send[s, :, 0:many] = real.T.astype(BF16)
            piece_send[s, :, many : 2 * many] = imag.T.astype(BF16)

        def total(s, side):
            first = pl.multiple_of((x * 2 + side) * rows, rows)
            value = piece_send[s, pl.ds(first, rows)].astype(F32)
            for d in range(1, across):
                first = pl.multiple_of(((d - 1) * 2 + side) * rows, rows)
                value = value + piece_land[s, pl.ds(first, rows)].astype(F32)
            return value

        def reduce_x(s):
            for d in range(1, across):
                piece_copy(s, d).wait_recv()

            @pl.when(s < passed)
            def _():
                half_send[s] = total(s, 1 - half).astype(BF16)
                half_copy(s).start()
                piece_held[s] = total(s, half)

            @pl.when(s >= passed)
            def _():
                for side in range(2):
                    last_send[s - passed, side] = total(s, half if side == 0 else 1 - half).astype(
                        BF16
                    )
                    last_copy(s - passed, side).start()

        def reduce_y(s):
            half_copy(s).wait_recv()
            back_send[s] = (piece_held[s] + half_land[s].astype(F32)).astype(BF16)
            back_copy(s).start()

        def one(s, carry):
            next_chunk(s)
            for here in quarters:
                weigh_turned(s, here)
            pieces(s, dot_nn(weighted_t[...], flat[...]))
            for d in range(1, across):
                piece_copy(s, d).start()

            @pl.when(s >= LAG_X)
            def _():
                reduce_x(s - LAG_X)

            @pl.when(jnp.logical_and(s >= LAG_Y, s < passed + LAG_Y))
            def _():
                reduce_y(s - LAG_Y)

            beside(s)
            return carry

        lax.fori_loop(0, final, one, 0)
        for q, here in enumerate(quarters):
            last_quarter(q).wait_recv()
            weigh_turned(final, here)
            both = dot_nn(weighted_t[:, here], flat[here, :])
            both = both if q == 0 else sums_t[...] + both
            if q < QUARTERS - 1:
                sums_t[...] = both
            else:
                pieces(final, both)
        for d in list(range(1, slabs, 2)) + list(range(0, slabs, 2)):
            home_copy(d).start()
        for s in range(final - LAG_X, final):
            reduce_x(s)
        for s in range(final - LAG_Y, passed):
            reduce_y(s)
        for s in range(passed):
            back_copy(s).wait_recv()
        for i in range(DIRECT):
            for side in range(2):
                last_copy(i, side).wait_recv()
        for d in range(slabs):
            home_copy(d).wait_recv()
        per = WIDTH // rows
        at_lane = lax.broadcasted_iota(jnp.int32, (rows, WIDTH), 1)

        def summed(chunk, part):
            here = slice(part * WIDTH, (part + 1) * WIDTH)
            if chunk < passed:
                return back_land[chunk, :, here].astype(F32)
            if chunk < final:
                both = [last_land[chunk - passed, side, :, here] for side in range(2)]
            else:
                both = [home_land[d, :, here] for d in range(slabs)]
            return sum(piece.astype(F32) for piece in both)

        for mode in range(MODES):
            for part in range(2):
                for q in range(bands // WIDTH):
                    value = jnp.zeros((rows, WIDTH), F32)
                    for t in range(per):
                        piece = summed(q * per + t, part)
                        shift = (t - mode) * rows % WIDTH
                        if shift:
                            piece = pltpu.roll(piece, shift, 1)
                        inside = (at_lane >= t * rows) & (at_lane < (t + 1) * rows)
                        value = jnp.where(inside, piece, value)
                    lane = (mode * 2 + part) * bands + q * WIDTH
                    out_ref[:, mode, part, q * WIDTH : (q + 1) * WIDTH] = (
                        value + nonlocal_sum[:, lane : lane + WIDTH]
                    )
        for s in range(slabs):
            if s < passed:
                back_copy(s).wait_send()
                half_copy(s).wait_send()
            elif s < final:
                last_copy(s - passed, 0).wait_send()
                last_copy(s - passed, 1).wait_send()
            for d in range(slabs):
                if s == final:
                    home_copy(d).wait_send()
                elif 0 < d < across:
                    piece_copy(s, d).wait_send()

    for q in range(QUARTERS):
        last_quarter(q).wait_send()
    for i in range(2):
        pl.semaphore_wait(paces.at[i], AHEAD - 1 + SLACK)
    for d in range(1, across):
        proj_x_copy(d).wait_send()
        gather_x(d, x).wait_send()
    proj_y_copy.wait_send()
    gather_y.wait_send()
    rows_copy.wait_send()


def body(
    wave_fields,
    potential_change,
    projectors,
    mode_vectors,
    coupling_base,
    coupling_change,
    projector_atom,
):
    own = wave_fields[0]
    points, _, bands = own.shape
    pools, slabs = lax.axis_size("ka"), lax.axis_size("ga")
    count = projectors.shape[1]
    atoms = mode_vectors.shape[-1]
    rows = bands // slabs
    across = slabs // 2
    columns = GROUPS * count
    wide = 2 * MODES * bands
    part_wide = 2 * MODES * rows
    vmem = pl.BlockSpec(memory_space=pltpu.VMEM)
    dma = pltpu.SemaphoreType.DMA
    result = pl.pallas_call(
        functools.partial(kernel, (pools, slabs, points, bands)),
        out_shape=jax.ShapeDtypeStruct((rows, MODES, 2, bands), F32),
        in_specs=[pl.BlockSpec(memory_space=pl.ANY)] * 7,
        out_specs=vmem,
        scratch_shapes=[
            pltpu.VMEM((bands // WIDTH, points, 2, WIDTH), BF16),
            pltpu.VMEM(potential_change.shape, BF16),
            pltpu.VMEM((columns, points), BF16),
            pltpu.VMEM((MODES * 6, atoms), F32),
            pltpu.VMEM(coupling_base.shape, F32),
            pltpu.VMEM(coupling_change.shape, F32),
            pltpu.VMEM((1, count), jnp.int32),
            pltpu.VMEM((2 * WIDTH, 2 * WIDTH), BF16),
            pltpu.VMEM((2 * MODES, points), F32),
            pltpu.VMEM((slabs, 2 * rows, points), BF16),
            pltpu.VMEM((points, 2 * bands), BF16),
            pltpu.VMEM((slabs, 2 * rows, points), BF16),
            pltpu.VMEM((points, wide), BF16),
            pltpu.VMEM((2 * MODES * rows, points), BF16),
            pltpu.VMEM((slabs, 2 * rows, columns), F32),
            pltpu.VMEM((across - 1, 2, 2 * rows, columns), F32),
            pltpu.VMEM((2 * rows, columns), F32),
            pltpu.VMEM((2 * rows, columns), F32),
            pltpu.VMEM((2, rows, columns), F32),
            pltpu.VMEM((2, bands, columns), F32),
            pltpu.VMEM((2, rows, columns), F32),
            pltpu.VMEM((2 * MODES * rows, columns), F32),
            pltpu.VMEM((rows, wide), F32),
            pltpu.VMEM((slabs, rows, wide), BF16),
            pltpu.VMEM((slabs, rows, wide), BF16),
            pltpu.VMEM((rows, wide), F32),
            pltpu.VMEM((rows, wide), BF16),
            pltpu.VMEM((rows, wide), BF16),
            pltpu.VMEM((slabs, bands, part_wide), BF16),
            pltpu.VMEM((slabs, (across - 1) * 2 * rows, part_wide), BF16),
            pltpu.VMEM((slabs, rows, part_wide), F32),
            pltpu.VMEM((slabs, rows, part_wide), BF16),
            pltpu.VMEM((slabs, rows, part_wide), BF16),
            pltpu.VMEM((slabs, rows, part_wide), BF16),
            pltpu.VMEM((slabs, rows, part_wide), BF16),
            pltpu.VMEM((DIRECT, 2, rows, part_wide), BF16),
            pltpu.VMEM((DIRECT, 2, rows, part_wide), BF16),
            pltpu.VMEM((slabs, rows, part_wide), BF16),
            pltpu.VMEM((2 * rows, wide), F32),
            pltpu.VMEM((part_wide, 2 * bands), F32),
            dma((2, slabs - 1 + QUARTERS)),
            dma((2, across)),
            dma((2, across)),
            dma((8,)),
            dma((2, slabs)),
            dma((2, slabs, across)),
            dma((2, slabs)),
            dma((2, slabs)),
            dma((2, DIRECT, 2)),
            dma((2, slabs)),
            dma((6,)),
            dma((2, QUARTERS)),
            pltpu.SemaphoreType.REGULAR((2,)),
        ],
        compiler_params=pltpu.CompilerParams(
            collective_id=0, has_side_effects=True, vmem_limit_bytes=58 << 20
        ),
        name="matrix_elements",
    )(
        own,
        potential_change,
        projectors.reshape(columns, points),
        mode_vectors.reshape(MODES * 6, atoms),
        coupling_base,
        coupling_change,
        projector_atom.reshape(1, count),
    )
    return result[None]


def solution(mesh):
    placed = (
        P("ka", "ga", None, None),
        P(None, None, "ga"),
        P(None, None, "ga"),
        P(),
        P(),
        P(),
        P(),
    )
    return jax.shard_map(
        body, mesh=mesh, in_specs=placed, out_specs=P("ka", "ga", None, None, None), check_vma=False
    )
```
